32 devices in a mesh: grp: 4 (over z), feat: 8 (over y, x, core).
Axes of the slice: x: 2, y: 2, z: 4, core: 2. Of those that a mesh axis runs over, the one named last changes fastest.
Arguments:
- features: bfloat16 [4, 192, 768, 128], P('grp', None, 'feat'), may hold values from -6 to 6
- adj_tiles: bfloat16 [4, 96, 128, 128], P('grp'), may hold values from -0.4375 to 0.4375
- tile_rows: int32 [4, 96], P('grp'), may hold values from 0 to 63, as said below
- tile_cols: int32 [4, 96], P('grp'), may hold values from 0 to 191
- self_blocks: int32 [4, 64], P('grp'), may hold values from 0 to 191, as said below
- weight: bfloat16 [1536, 1024], replicated, may hold values from -0.15625 to 0.15625
- proj_bias: float32 [1024], replicated, may hold values from -0.5 to 0.5
- cotangent: bfloat16 [4, 8192, 1024], P('grp', 'feat'), may hold values from -0.03125 to 0.03125
Outputs:
- hidden: bfloat16 [4, 8192, 1024], P('grp', 'feat')
- weight_grad: float32 [1536, 1024], P('feat')
The draws below stay inside these ranges and needn't reach their ends.
Inputs may be any that keep to these rules, and one draw needn't show every extreme that they name: `tile_rows`: within each minibatch the row blocks are in nondecreasing order and every row block 0 to 63 has at least one tile. `self_blocks`: within each minibatch the blocks are distinct.
All inputs are finite; a program needn't handle non-finite values.
Results may differ from the reference program's by a relative error of at most 0.0038.
Values may be sent and summed in bfloat16 or wider, within the bound.
A program may use at most 128 MiB of HBM per device.

```python
import jax
import jax.numpy as jnp
from jax import lax

F = 768
HID = 1024
TILE = 128
GROUPS = 4
NDST = 8192
NRB = 64
NT = 96
NCB = 192


def draw_tile_rows(key, part):

    def one_group(group_key):
        key_one, key_two, key_three = jax.random.split(group_key, 3)
        extra_count = NT - NRB
        first = jax.random.randint(key_one, (extra_count,), 0, NRB)
        second = jax.random.randint(key_two, (extra_count,), 0, NRB)
        third = jax.random.randint(key_three, (extra_count,), 0, NRB)
        skewed = jnp.minimum(jnp.minimum(first, second), third).astype(jnp.int32)
        every_block = jnp.arange(NRB, dtype=jnp.int32)
        return jnp.sort(jnp.concatenate([every_block, skewed]))
    return jax.vmap(one_group)(jax.random.split(jax.random.fold_in(key, 11), GROUPS)).astype(jnp.int32)


def draw_self_blocks(key, part):

    def one_group(group_key):
        key_one, key_two = jax.random.split(group_key, 2)
        middle = jax.random.permutation(key_one, NCB - 2)[:NRB - 2].astype(jnp.int32) + 1
        ends = jnp.array([0, NCB - 1], dtype=jnp.int32)
        chosen = jnp.concatenate([middle, ends])
        order = jax.random.permutation(key_two, NRB)
        return chosen[order]
    return jax.vmap(one_group)(jax.random.split(jax.random.fold_in(key, 23), GROUPS)).astype(jnp.int32)


def with_ends(entries, rng, smallest, high):
    longest = entries.shape.index(max(entries.shape))
    spots = []
    for shift in (0, 1):
        where = [jax.random.randint(jax.random.fold_in(rng, axis), (), 0, length) for axis, length in enumerate(entries.shape)]
        where[longest] = (where[longest] + shift) % entries.shape[longest]
        spots.append(tuple(where))
    return entries.at[spots[0]].set(smallest).at[spots[1]].set(high)


def level_of(key, shape, cuts, least, high):
    loudness = 1.0
    for dim, blocks in cuts:
        heights = jax.random.uniform(jax.random.fold_in(jax.random.fold_in(key, 6), dim), (blocks,), jnp.float32, least / len(cuts), high / len(cuts))
        loudness = loudness * jnp.repeat(jnp.exp(heights), shape[dim] // blocks).reshape((-1,) + (1,) * (len(shape) - 1 - dim))
    return loudness


def noise(rng, shape, scale, bound, pieces=(), held_as=jnp.bfloat16):
    loudness = level_of(rng, shape, pieces, -0.22, 0.18) if pieces else 1.0
    result = jax.random.normal(rng, shape, jnp.float32) * scale * loudness
    return jnp.minimum(jnp.maximum(result, -bound), bound).astype(held_as)


def setup_inputs(seed: int = 0) -> dict:
    seeds = jax.random.split(jax.random.key(seed), 9)
    features = noise(seeds[0], (GROUPS, NCB, F, TILE), 1.0, 6.0, ((0, 4), (2, 8)))
    adj_tiles = noise(seeds[1], (GROUPS, NT, TILE, TILE), (TILE * NT // NRB) ** -0.5, 0.4375, ((0, 4),))
    tile_rows = draw_tile_rows(jax.random.fold_in(seeds[8], 71), 0)
    tile_cols = with_ends(jax.random.randint(seeds[3], (GROUPS, NT), 0, NCB), jax.random.fold_in(seeds[3], 1), 0, NCB - 1).astype(jnp.int32)
    self_blocks = draw_self_blocks(jax.random.fold_in(seeds[8], 71), 0)
    weight = noise(seeds[5], (2 * F, HID), (2 * F) ** -0.5, 0.15625)
    proj_bias = jnp.clip(jax.random.uniform(seeds[6], (HID,), jnp.float32, -0.5, 0.5), -0.5, 0.5)
    cotangent = noise(seeds[7], (GROUPS, NDST, HID), (GROUPS * NDST) ** -0.5, 0.03125, ((0, 4), (1, 8)))
    return dict(features=features, adj_tiles=adj_tiles, tile_rows=tile_rows, tile_cols=tile_cols, self_blocks=self_blocks, weight=weight, proj_bias=proj_bias, cotangent=cotangent)


def elu_act(value):
    return jnp.where(value > 0, value, jnp.expm1(jnp.minimum(value, 0.0)))


def combine_group(features_g, tiles_g, rows_g, cols_g, blocks_g):
    picked = jnp.take(features_g, cols_g, axis=0).astype(jnp.float32)
    contrib = jnp.einsum("tfs,tds->tfd", picked, tiles_g.astype(jnp.float32))
    summed = jax.ops.segment_sum(contrib, rows_g, num_segments=NRB)
    aggregate = summed.astype(jnp.bfloat16)
    self_feat = jnp.take(features_g, blocks_g, axis=0)
    return jnp.concatenate([self_feat, aggregate], axis=1)


def reference(features, adj_tiles, tile_rows, tile_cols, self_blocks, weight, proj_bias, cotangent):
    def step_group(carry, inputs):
        features_g, tiles_g, rows_g, cols_g, blocks_g, cot_g = inputs
        combined = combine_group(features_g, tiles_g, rows_g, cols_g, blocks_g)
        preact = jnp.einsum("rcd,ch->rdh", combined.astype(jnp.float32), weight.astype(jnp.float32))
        preact = preact.reshape(NDST, HID) + proj_bias
        hidden_g = elu_act(preact).astype(jnp.bfloat16)
        pre_grad = (cot_g.astype(jnp.float32) * jnp.exp(jnp.minimum(preact, 0.0))).astype(jnp.bfloat16)
        grad_part = jnp.einsum("rcd,rdh->ch", combined.astype(jnp.float32), pre_grad.reshape(NRB, TILE, HID).astype(jnp.float32))
        return carry + grad_part, hidden_g

    start = jnp.zeros((2 * F, HID), jnp.float32)
    weight_grad, hidden = lax.scan(step_group, start, (features, adj_tiles, tile_rows, tile_cols, self_blocks, cotangent))
    return hidden, weight_grad
```

```python
import functools

import jax
import jax.numpy as jnp
from jax import lax
from jax.experimental import pallas as pl
from jax.experimental.pallas import tpu as pltpu
from jax.sharding import PartitionSpec as P

MESH = pl.DeviceIdType.MESH
PIECES = 3
VMEM_BYTES = 56 * 1024 * 1024


def exchange_kernel(
    n, cols_ref, keep_ref, last_ref, blocks_ref, feat_ref, adj_ref, comb_ref,
    sendbuf, recvbuf, scan, send_sem, recv_sem,
):
    me = lax.axis_index("feat")
    rows = sendbuf.shape[2]
    width = feat_ref.shape[1]
    tiles = adj_ref.shape[0]

    barrier = pltpu.get_barrier_semaphore()

    def greet(i, carry):
        pl.semaphore_signal(
            barrier, inc=1, device_id={"feat": lax.rem(me + i, n)}, device_id_type=MESH
        )
        return carry

    lax.fori_loop(1, n, greet, 0)

    def fill_self(i, carry):
        peer = lax.rem(me + i, n)
        for r in range(rows):
            sendbuf[i, 0, r] = feat_ref[blocks_ref[peer * rows + r]]
        return carry

    def copy_to(i, kind):
        return pltpu.make_async_remote_copy(
            src_ref=sendbuf.at[i, kind],
            dst_ref=recvbuf.at[me, kind],
            send_sem=send_sem.at[i, kind],
            recv_sem=recv_sem.at[me, kind],
            device_id={"feat": lax.rem(me + i, n)},
            device_id_type=MESH,
        )

    def send_self(i, carry):
        fill_self(i, carry)
        copy_to(i, 0).start()
        return carry

    fill_self(1, 0)
    pl.semaphore_wait(barrier, n - 1)
    copy_to(1, 0).start()
    lax.fori_loop(2, n, send_self, 0)
    for r in range(rows):
        recvbuf[me, 0, r] = feat_ref[blocks_ref[me * rows + r]]

    def tile_terms(step, carry):
        for k in range(8):
            t = step * 8 + k
            scan[t] = lax.dot_general(
                feat_ref[cols_ref[t]], adj_ref[t], (((1,), (1,)), ((), ())),
                preferred_element_type=jnp.float32,
            )
        return carry

    lax.fori_loop(0, tiles // 8, tile_terms, 0)

    def running_sums(step, acc):
        for k in range(8):
            t = step * 8 + k
            acc = scan[t] + keep_ref[t] * acc
            scan[t] = acc
        return acc

    lax.fori_loop(0, tiles // 8, running_sums, jnp.zeros((width, 128), jnp.float32))

    def send_agg(i, carry):
        peer = lax.rem(me + i, n)
        for r in range(rows):
            sendbuf[i, 1, r] = scan[last_ref[peer * rows + r]].astype(jnp.bfloat16)
        copy_to(i, 1).start()
        return carry

    lax.fori_loop(1, n, send_agg, 0)
    for r in range(rows):
        recvbuf[me, 1, r] = scan[last_ref[me * rows + r]].astype(jnp.bfloat16)

    def wait_in(i, carry):
        src = lax.rem(me - i + n, n)
        for kind in range(2):
            pltpu.make_async_remote_copy(
                src_ref=sendbuf.at[i, kind],
                dst_ref=recvbuf.at[src, kind],
                send_sem=send_sem.at[i, kind],
                recv_sem=recv_sem.at[src, kind],
                device_id={"feat": lax.rem(me + i, n)},
                device_id_type=MESH,
            ).wait_recv()
        return carry

    lax.fori_loop(1, n, wait_in, 0)

    for kind in range(2):
        base = kind * n * width
        for r in range(rows):
            lanes = pl.ds(r * 128, 128)
            if width % 16 == 0:
                for src in range(n):
                    comb_ref[pl.ds(base + src * width, width), lanes] = recvbuf[src, kind, r]
            else:
                whole = jnp.concatenate(
                    [recvbuf[src, kind, r].astype(jnp.float32) for src in range(n)], axis=0
                )
                comb_ref[pl.ds(base, n * width), lanes] = whole.astype(jnp.bfloat16)

    def wait_out(i, carry):
        for kind in range(2):
            copy_to(i, kind).wait_send()
        return carry

    lax.fori_loop(1, n, wait_out, 0)


def layer_kernel(
    n, nz, comb_ref, w_ref, bias_ref, cot_ref, hid_ref, grad_ref,
    pg, lhs, picked, mine, pair_out, pair_in, own, chip_out, chip_in, red, z_out, z_in, g_out, g_in,
    pair_sem, chip_ssem, chip_rsem, z_ssem, z_rsem, g_ssem, g_rsem,
):
    me = lax.axis_index("feat")
    mz = lax.axis_index("grp")
    nc = n // 2
    chip, core = me // 2, lax.rem(me, 2)
    sibling = chip * 2 + (1 - core)
    share = grad_ref.shape[0]
    piece = share // PIECES
    hid = grad_ref.shape[1]
    cw = hid // nz

    def chip_at(i):
        return lax.rem(chip + i, nc) * 2 + core

    def z_at(i):
        return lax.rem(mz + i, nz)

    barrier = pltpu.get_barrier_semaphore()
    pl.semaphore_signal(barrier, inc=1, device_id={"feat": sibling}, device_id_type=MESH)
    for i in range(1, nc):
        pl.semaphore_signal(barrier, inc=1, device_id={"feat": chip_at(i)}, device_id_type=MESH)
    for i in range(1, nz):
        pl.semaphore_signal(barrier, inc=1, device_id={"grp": z_at(i)}, device_id_type=MESH)

    nodes = comb_ref.shape[1]
    step_nodes = 256
    step_cols = 256

    def forward(step, carry):
        at = pl.ds(pl.multiple_of(step * step_nodes, step_nodes), step_nodes)
        lhs[...] = comb_ref[:, at].T

        def forward_columns(k, inner):
            some = pl.ds(pl.multiple_of(k * step_cols, step_cols), step_cols)
            pre = jnp.dot(lhs[...], w_ref[:, some], preferred_element_type=jnp.float32)
            pre = pre + bias_ref[:, some]
            decay = jnp.exp(jnp.minimum(pre, 0.0))
            hid_ref[at, some] = jnp.where(pre > 0, pre, decay - 1.0).astype(jnp.bfloat16)
            pg[at, some] = (cot_ref[at, some].astype(jnp.float32) * decay).astype(jnp.bfloat16)
            return inner

        return lax.fori_loop(0, hid // step_cols, forward_columns, carry)

    lax.fori_loop(0, nodes // step_nodes, forward, 0)
    pl.semaphore_wait(barrier, 1 + (nc - 1) + (nz - 1))

    def terms(p, parity, out):
        for i in range(nc):
            owner = lax.rem(chip + i, nc) * 2 + parity
            at = pl.multiple_of(owner * share + p * piece, piece)
            picked[i * piece:(i + 1) * piece] = comb_ref[pl.ds(at, piece), :]

        def some_columns(k, carry):
            some = pl.ds(pl.multiple_of(k * step_cols, step_cols), step_cols)
            out[:, some] = jnp.dot(
                picked[...], pg[:, some], preferred_element_type=jnp.float32
            )
            return carry

        lax.fori_loop(0, hid // step_cols, some_columns, 0)

    def pair_copy(p):
        return pltpu.make_async_remote_copy(
            src_ref=pair_out.at[p], dst_ref=pair_in.at[p],
            send_sem=pair_sem.at[p, 0], recv_sem=pair_sem.at[p, 1],
            device_id={"feat": sibling}, device_id_type=MESH,
        )

    def chip_copy(p, i):
        return pltpu.make_async_remote_copy(
            src_ref=chip_out.at[p, i - 1], dst_ref=chip_in.at[p, i - 1],
            send_sem=chip_ssem.at[p, i - 1], recv_sem=chip_rsem.at[p, i - 1],
            device_id={"feat": chip_at(i)}, device_id_type=MESH,
        )

    def z_copy(p, i):
        return pltpu.make_async_remote_copy(
            src_ref=z_out.at[p, i - 1], dst_ref=z_in.at[p, i - 1],
            send_sem=z_ssem.at[p, i - 1], recv_sem=z_rsem.at[p, i - 1],
            device_id={"grp": z_at(i)}, device_id_type=MESH,
        )

    def g_copy(p, i):
        return pltpu.make_async_remote_copy(
            src_ref=g_out.at[p], dst_ref=g_in.at[p, i - 1],
            send_sem=g_ssem.at[p, i - 1], recv_sem=g_rsem.at[p, i - 1],
            device_id={"grp": z_at(i)}, device_id_type=MESH,
        )

    def columns(z):
        return pl.ds(pl.multiple_of(z * cw, cw), cw)

    def pair_stage(p):
        terms(p, 1 - core, pair_out.at[p])
        pair_copy(p).start()

    def chip_stage(p):
        terms(p, core, mine)
        pair_copy(p).wait_recv()
        own[p] = mine[:piece] + pair_in[p, :piece]
        for i in range(1, nc):
            part = pl.ds(i * piece, piece)
            chip_out[p, i - 1] = (mine[part] + pair_in[p, part]).astype(jnp.bfloat16)
            chip_copy(p, i).start()

    def z_stage(p):
        total = own[p]
        for i in range(1, nc):
            chip_copy(p, i).wait_recv()
            total = total + chip_in[p, i - 1].astype(jnp.float32)
        red[p] = total
        for i in range(1, nz):
            z_out[p, i - 1] = red[p, :, columns(z_at(i))].astype(jnp.bfloat16)
            z_copy(p, i).start()

    def g_stage(p):
        total = red[p, :, columns(mz)]
        for i in range(1, nz):
            z_copy(p, i).wait_recv()
            total = total + z_in[p, i - 1].astype(jnp.float32)
        g_out[p] = total.astype(jnp.bfloat16)
        for i in range(1, nz):
            g_copy(p, i).start()
        grad_ref[pl.ds(p * piece, piece), columns(mz)] = g_out[p].astype(jnp.float32)

    def last_stage(p):
        for i in range(1, nz):
            g_copy(p, i).wait_recv()
            grad_ref[pl.ds(p * piece, piece), columns(lax.rem(mz - i + nz, nz))] = (
                g_in[p, i - 1].astype(jnp.float32)
            )

    pair_stage(0)
    pair_stage(1)
    chip_stage(0)
    pair_stage(2)
    chip_stage(1)
    chip_stage(2)
    z_stage(0)
    z_stage(1)
    g_stage(0)
    z_stage(2)
    g_stage(1)
    g_stage(2)
    for p in range(PIECES):
        last_stage(p)
    for p in range(PIECES):
        pair_copy(p).wait_send()
        for i in range(1, nc):
            chip_copy(p, i).wait_send()
        for i in range(1, nz):
            z_copy(p, i).wait_send()
            g_copy(p, i).wait_send()


def per_device(
    n, nz,
    features, adj_tiles, tile_rows, tile_cols, self_blocks, weight, proj_bias, cotangent,
):
    feats = features[0]
    width, side = feats.shape[1], feats.shape[2]
    tiles = adj_tiles.shape[1]
    block_count = self_blocks.shape[1]
    rows = block_count // n
    depth, hid = weight.shape
    nodes = rows * side
    share = depth // n
    piece = share // PIECES
    nc = n // 2
    cw = hid // nz

    row_of = tile_rows[0]
    keep = jnp.concatenate(
        [jnp.zeros((1,), jnp.float32), (row_of[1:] == row_of[:-1]).astype(jnp.float32)]
    )
    last = jnp.sum(
        (row_of[None, :] <= jnp.arange(block_count, dtype=jnp.int32)[:, None]).astype(jnp.int32),
        axis=1,
    ) - 1

    smem = pl.BlockSpec(memory_space=pltpu.SMEM)
    vmem = pl.BlockSpec(memory_space=pltpu.VMEM)
    combined = pl.pallas_call(
        functools.partial(exchange_kernel, n),
        out_shape=jax.ShapeDtypeStruct((depth, nodes), jnp.bfloat16),
        in_specs=[smem] * 4 + [vmem] * 2,
        out_specs=vmem,
        scratch_shapes=[
            pltpu.VMEM((n, 2, rows, width, side), jnp.bfloat16),
            pltpu.VMEM((n, 2, rows, width, side), jnp.bfloat16),
            pltpu.VMEM((tiles, width, side), jnp.float32),
            pltpu.SemaphoreType.DMA((n, 2)),
            pltpu.SemaphoreType.DMA((n, 2)),
        ],
        compiler_params=pltpu.CompilerParams(
            collective_id=0, has_side_effects=True, vmem_limit_bytes=VMEM_BYTES
        ),
        name="exchange",
    )(tile_cols[0], keep, last, self_blocks[0], feats, adj_tiles[0])

    dma = pltpu.SemaphoreType.DMA
    hidden, weight_grad = pl.pallas_call(
        functools.partial(layer_kernel, n, nz),
        out_shape=(
            jax.ShapeDtypeStruct((nodes, hid), jnp.bfloat16),
            jax.ShapeDtypeStruct((share, hid), jnp.float32),
        ),
        in_specs=[vmem] * 4,
        out_specs=(vmem, vmem),
        scratch_shapes=[
            pltpu.VMEM((nodes, hid), jnp.bfloat16),
            pltpu.VMEM((256, depth), jnp.bfloat16),
            pltpu.VMEM((nc * piece, nodes), jnp.bfloat16),
            pltpu.VMEM((nc * piece, hid), jnp.float32),
            pltpu.VMEM((PIECES, nc * piece, hid), jnp.float32),
            pltpu.VMEM((PIECES, nc * piece, hid), jnp.float32),
            pltpu.VMEM((PIECES, piece, hid), jnp.float32),
            pltpu.VMEM((PIECES, nc - 1, piece, hid), jnp.bfloat16),
            pltpu.VMEM((PIECES, nc - 1, piece, hid), jnp.bfloat16),
            pltpu.VMEM((PIECES, piece, hid), jnp.float32),
            pltpu.VMEM((PIECES, nz - 1, piece, cw), jnp.bfloat16),
            pltpu.VMEM((PIECES, nz - 1, piece, cw), jnp.bfloat16),
            pltpu.VMEM((PIECES, piece, cw), jnp.bfloat16),
            pltpu.VMEM((PIECES, nz - 1, piece, cw), jnp.bfloat16),
            dma((PIECES, 2)),
            dma((PIECES, nc - 1)),
            dma((PIECES, nc - 1)),
            dma((PIECES, nz - 1)),
            dma((PIECES, nz - 1)),
            dma((PIECES, nz - 1)),
            dma((PIECES, nz - 1)),
        ],
        compiler_params=pltpu.CompilerParams(
            collective_id=1, has_side_effects=True, vmem_limit_bytes=VMEM_BYTES
        ),
        name="layer",
    )(combined, weight, proj_bias[None], cotangent[0])
    return (hidden[None], weight_grad)


def solution(mesh):
    return jax.shard_map(
        functools.partial(per_device, mesh.shape["feat"], mesh.shape["grp"]),
        mesh=mesh,
        in_specs=(
            P("grp", None, "feat", None),
            P("grp", None, None, None),
            P("grp", None),
            P("grp", None),
            P("grp", None),
            P(),
            P(),
            P("grp", "feat", None),
        ),
        out_specs=(P("grp", "feat", None), P("feat", None)),
        check_vma=False,
    )
```

```python
import functools

import jax
import jax.numpy as jnp
from jax import lax
from jax.experimental import pallas as pl
from jax.experimental.pallas import tpu as pltpu
from jax.sharding import PartitionSpec as P

MESH = pl.DeviceIdType.MESH
PIECES = 3
GROUP = 2
VMEM_BYTES = 60 * 1024 * 1024


def layer_kernel(
    n, nz, rows_ref, cols_ref, blocks_ref, feat_hbm, adj_hbm, w_hbm, bias_ref, cot_hbm,
    hid_hbm, grad_ref,
    feat, adj, w, cot, hidden, sendbuf, recvbuf, scan, last, comb_ref,
    pg, lhs, picked, mine, pair_out, pair_in, own, chip_out, chip_in, red,
    z_out, z_in, g_out, g_in,
    load_sem, hid_sem, send_sem, recv_sem,
    pair_sem, chip_ssem, chip_rsem, z_ssem, z_rsem, g_ssem, g_rsem,
):
    me = lax.axis_index("feat")
    mz = lax.axis_index("grp")
    nc = n // 2
    chip, core = me // 2, lax.rem(me, 2)
    sibling = chip * 2 + (1 - core)
    share, hid = grad_ref.shape
    piece = share // PIECES
    cw = hid // nz
    rows = sendbuf.shape[2]
    width = feat.shape[1]
    tiles = adj.shape[0]
    groups = rows // GROUP
    step_nodes = GROUP * 128
    step_cols = 256

    def chip_at(i):
        return lax.rem(chip + i, nc) * 2 + core

    def z_at(i):
        return lax.rem(mz + i, nz)

    loads = [
        pltpu.make_async_copy(src, dst, load_sem.at[k])
        for k, (src, dst) in enumerate(
            [(feat_hbm, feat), (adj_hbm, adj), (w_hbm, w), (cot_hbm, cot)]
        )
    ]
    for load in loads:
        load.start()

    barrier = pltpu.get_barrier_semaphore()

    def greet(i, carry):
        pl.semaphore_signal(
            barrier, inc=1, device_id={"feat": lax.rem(me + i, n)}, device_id_type=MESH
        )
        return carry

    lax.fori_loop(1, n, greet, 0)
    for i in range(1, nz):
        pl.semaphore_signal(barrier, inc=1, device_id={"grp": z_at(i)}, device_id_type=MESH)

    def fill_self(i, carry):
        peer = lax.rem(me + i, n)
        for r in range(rows):
            sendbuf[i, 0, r] = feat[blocks_ref[peer * rows + r]]
        return carry

    def self_copy(i, src):
        return pltpu.make_async_remote_copy(
            src_ref=sendbuf.at[i, 0],
            dst_ref=recvbuf.at[src, 0],
            send_sem=send_sem.at[i, 0],
            recv_sem=recv_sem.at[src, 0],
            device_id={"feat": lax.rem(me + i, n)},
            device_id_type=MESH,
        )

    def agg_copy(i, q, src):
        some = pl.ds(q * GROUP, GROUP)
        return pltpu.make_async_remote_copy(
            src_ref=sendbuf.at[i, 1, some],
            dst_ref=recvbuf.at[src, 1, some],
            send_sem=send_sem.at[i, 1 + q],
            recv_sem=recv_sem.at[src, 1 + q],
            device_id={"feat": lax.rem(me + i, n)},
            device_id_type=MESH,
        )

    def send_self(i, carry):
        fill_self(i, carry)
        self_copy(i, me).start()
        return carry

    loads[0].wait()
    fill_self(1, 0)
    pl.semaphore_wait(barrier, (n - 1) + (nz - 1))
    self_copy(1, me).start()
    lax.fori_loop(2, n, send_self, 0)
    for r in range(rows):
        recvbuf[me, 0, r] = feat[blocks_ref[me * rows + r]]

    loads[1].wait()

    def tile_terms(step, carry):
        for k in range(8):
            t = step * 8 + k
            scan[t] = lax.dot_general(
                feat[cols_ref[t]], adj[t], (((1,), (1,)), ((), ())),
                preferred_element_type=jnp.float32,
            )
        return carry

    lax.fori_loop(0, tiles // 8, tile_terms, 0)

    def running_sums(step, acc):
        for k in range(8):
            t = step * 8 + k
            same = rows_ref[t] == rows_ref[jnp.maximum(t - 1, 0)]
            acc = scan[t] + jnp.where(same, 1.0, 0.0) * acc
            scan[t] = acc
        return acc

    lax.fori_loop(0, tiles // 8, running_sums, jnp.zeros((width, 128), jnp.float32))

    def find_last(r, carry):
        at = jnp.int32(0)
        step = 1 << (tiles.bit_length() - 1)
        while step:
            there = at + step
            fits = (there < tiles) & (rows_ref[jnp.minimum(there, tiles - 1)] <= r)
            at = jnp.where(fits, there, at)
            step //= 2
        last[r] = at
        return carry

    lax.fori_loop(0, n * rows, find_last, 0)

    def send_group(q, carry):
        def send_agg(i, inner):
            peer = lax.rem(me + i, n)
            for k in range(GROUP):
                r = q * GROUP + k
                sendbuf[i, 1, r] = scan[last[peer * rows + r]].astype(jnp.bfloat16)
            agg_copy(i, q, me).start()
            return inner

        return lax.fori_loop(1, n, send_agg, carry)

    lax.fori_loop(0, groups, send_group, 0)
    for r in range(rows):
        recvbuf[me, 1, r] = scan[last[me * rows + r]].astype(jnp.bfloat16)

    loads[2].wait()
    loads[3].wait()

    def wait_self(i, carry):
        self_copy(i, lax.rem(me - i + n, n)).wait_recv()
        return carry

    lax.fori_loop(1, n, wait_self, 0)

    def hid_copy(q):
        at = pl.ds(pl.multiple_of(q * step_nodes, step_nodes), step_nodes)
        return pltpu.make_async_copy(hidden.at[at], hid_hbm.at[at], hid_sem.at[q])

    def forward(q, carry):
        def wait_agg(i, inner):
            agg_copy(i, q, lax.rem(me - i + n, n)).wait_recv()
            return inner

        lax.fori_loop(1, n, wait_agg, 0)
        for kind in range(2):
            base = kind * n * width
            for k in range(GROUP):
                r = q * GROUP + k
                lanes = pl.ds(pl.multiple_of(r * 128, 128), 128)
                if width % 16 == 0:
                    for src in range(n):
                        comb_ref[pl.ds(base + src * width, width), lanes] = recvbuf[src, kind, r]
                else:
                    whole = jnp.concatenate(
                        [recvbuf[src, kind, r].astype(jnp.float32) for src in range(n)], axis=0
                    )
                    comb_ref[pl.ds(base, n * width), lanes] = whole.astype(jnp.bfloat16)

        at = pl.ds(pl.multiple_of(q * step_nodes, step_nodes), step_nodes)
        lhs[...] = comb_ref[:, at].T

        def forward_columns(k, inner):
            some = pl.ds(pl.multiple_of(k * step_cols, step_cols), step_cols)
            pre = jnp.dot(lhs[...], w[:, some], preferred_element_type=jnp.float32)
            pre = pre + bias_ref[:, some]
            decay = jnp.exp(jnp.minimum(pre, 0.0))
            hidden[at, some] = jnp.where(pre > 0, pre, decay - 1.0).astype(jnp.bfloat16)
            pg[at, some] = (cot[at, some].astype(jnp.float32) * decay).astype(jnp.bfloat16)
            return inner

        lax.fori_loop(0, hid // step_cols, forward_columns, 0)
        hid_copy(q).start()
        return carry

    lax.fori_loop(0, groups, forward, 0)

    def terms(p, parity, out):
        for i in range(nc):
            owner = lax.rem(chip + i, nc) * 2 + parity
            at = pl.multiple_of(owner * share + p * piece, piece)
            picked[i * piece:(i + 1) * piece] = comb_ref[pl.ds(at, piece), :]

        def some_columns(k, carry):
            some = pl.ds(pl.multiple_of(k * step_cols, step_cols), step_cols)
            out[:, some] = jnp.dot(
                picked[...], pg[:, some], preferred_element_type=jnp.float32
            )
            return carry

        lax.fori_loop(0, hid // step_cols, some_columns, 0)

    def pair_copy(p):
        return pltpu.make_async_remote_copy(
            src_ref=pair_out.at[p], dst_ref=pair_in.at[p],
            send_sem=pair_sem.at[p, 0], recv_sem=pair_sem.at[p, 1],
            device_id={"feat": sibling}, device_id_type=MESH,
        )

    def chip_copy(p, i):
        return pltpu.make_async_remote_copy(
            src_ref=chip_out.at[p, i - 1], dst_ref=chip_in.at[p, i - 1],
            send_sem=chip_ssem.at[p, i - 1], recv_sem=chip_rsem.at[p, i - 1],
            device_id={"feat": chip_at(i)}, device_id_type=MESH,
        )

    def z_copy(p, i):
        return pltpu.make_async_remote_copy(
            src_ref=z_out.at[p, i - 1], dst_ref=z_in.at[p, i - 1],
            send_sem=z_ssem.at[p, i - 1], recv_sem=z_rsem.at[p, i - 1],
            device_id={"grp": z_at(i)}, device_id_type=MESH,
        )

    def g_copy(p, i):
        return pltpu.make_async_remote_copy(
            src_ref=g_out.at[p], dst_ref=g_in.at[p, i - 1],
            send_sem=g_ssem.at[p, i - 1], recv_sem=g_rsem.at[p, i - 1],
            device_id={"grp": z_at(i)}, device_id_type=MESH,
        )

    def columns(z):
        return pl.ds(pl.multiple_of(z * cw, cw), cw)

    def pair_stage(p):
        terms(p, 1 - core, pair_out.at[p])
        pair_copy(p).start()

    def chip_stage(p):
        terms(p, core, mine)
        pair_copy(p).wait_recv()
        own[p] = mine[:piece] + pair_in[p, :piece]
        for i in range(1, nc):
            part = pl.ds(i * piece, piece)
            chip_out[p, i - 1] = (mine[part] + pair_in[p, part]).astype(jnp.bfloat16)
            chip_copy(p, i).start()

    def z_stage(p):
        total = own[p]
        for i in range(1, nc):
            chip_copy(p, i).wait_recv()
            total = total + chip_in[p, i - 1].astype(jnp.float32)
        red[p] = total
        for i in range(1, nz):
            z_out[p, i - 1] = red[p, :, columns(z_at(i))].astype(jnp.bfloat16)
            z_copy(p, i).start()

    def g_stage(p):
        total = red[p, :, columns(mz)]
        for i in range(1, nz):
            z_copy(p, i).wait_recv()
            total = total + z_in[p, i - 1].astype(jnp.float32)
        g_out[p] = total.astype(jnp.bfloat16)
        for i in range(1, nz):
            g_copy(p, i).start()
        grad_ref[pl.ds(p * piece, piece), columns(mz)] = g_out[p]

    def last_stage(p):
        for i in range(1, nz):
            g_copy(p, i).wait_recv()
            grad_ref[pl.ds(p * piece, piece), columns(lax.rem(mz - i + nz, nz))] = g_in[p, i - 1]

    pair_stage(0)
    pair_stage(1)
    chip_stage(0)
    pair_stage(2)
    chip_stage(1)
    chip_stage(2)
    z_stage(0)
    z_stage(1)
    g_stage(0)
    z_stage(2)
    g_stage(1)
    g_stage(2)
    for p in range(PIECES):
        last_stage(p)
    for p in range(PIECES):
        pair_copy(p).wait_send()
        for i in range(1, nc):
            chip_copy(p, i).wait_send()
        for i in range(1, nz):
            z_copy(p, i).wait_send()
            g_copy(p, i).wait_send()

    def wait_out(i, carry):
        self_copy(i, me).wait_send()
        for q in range(groups):
            agg_copy(i, q, me).wait_send()
        return carry

    lax.fori_loop(1, n, wait_out, 0)
    for q in range(groups):
        hid_copy(q).wait()


def per_device(
    n, nz,
    features, adj_tiles, tile_rows, tile_cols, self_blocks, weight, proj_bias, cotangent,
):
    feats, adj = features[0], adj_tiles[0]
    width, side = feats.shape[1], feats.shape[2]
    tiles = adj.shape[0]
    block_count = self_blocks.shape[1]
    rows = block_count // n
    depth, hid = weight.shape
    nodes = rows * side
    share = depth // n
    piece = share // PIECES
    nc = n // 2
    cw = hid // nz
    groups = rows // GROUP
    step_nodes = GROUP * side

    smem = pl.BlockSpec(memory_space=pltpu.SMEM)
    vmem = pl.BlockSpec(memory_space=pltpu.VMEM)
    anywhere = pl.BlockSpec(memory_space=pl.ANY)
    dma = pltpu.SemaphoreType.DMA
    hidden, weight_grad = pl.pallas_call(
        functools.partial(layer_kernel, n, nz),
        out_shape=(
            jax.ShapeDtypeStruct((nodes, hid), jnp.bfloat16),
            jax.ShapeDtypeStruct((share, hid), jnp.bfloat16),
        ),
        in_specs=[smem] * 3 + [anywhere] * 3 + [vmem, anywhere],
        out_specs=(anywhere, vmem),
        scratch_shapes=[
            pltpu.VMEM(feats.shape, jnp.bfloat16),
            pltpu.VMEM(adj.shape, jnp.bfloat16),
            pltpu.VMEM(weight.shape, jnp.bfloat16),
            pltpu.VMEM((nodes, hid), jnp.bfloat16),
            pltpu.VMEM((nodes, hid), jnp.bfloat16),
            pltpu.VMEM((n, 2, rows, width, side), jnp.bfloat16),
            pltpu.VMEM((n, 2, rows, width, side), jnp.bfloat16),
            pltpu.VMEM((tiles, width, side), jnp.float32),
            pltpu.SMEM((block_count,), jnp.int32),
            pltpu.VMEM((depth, nodes), jnp.bfloat16),
            pltpu.VMEM((nodes, hid), jnp.bfloat16),
            pltpu.VMEM((step_nodes, depth), jnp.bfloat16),
            pltpu.VMEM((nc * piece, nodes), jnp.bfloat16),
            pltpu.VMEM((nc * piece, hid), jnp.float32),
            pltpu.VMEM((PIECES, nc * piece, hid), jnp.float32),
            pltpu.VMEM((PIECES, nc * piece, hid), jnp.float32),
            pltpu.VMEM((PIECES, piece, hid), jnp.float32),
            pltpu.VMEM((PIECES, nc - 1, piece, hid), jnp.bfloat16),
            pltpu.VMEM((PIECES, nc - 1, piece, hid), jnp.bfloat16),
            pltpu.VMEM((PIECES, piece, hid), jnp.float32),
            pltpu.VMEM((PIECES, nz - 1, piece, cw), jnp.bfloat16),
            pltpu.VMEM((PIECES, nz - 1, piece, cw), jnp.bfloat16),
            pltpu.VMEM((PIECES, piece, cw), jnp.bfloat16),
            pltpu.VMEM((PIECES, nz - 1, piece, cw), jnp.bfloat16),
            dma((4,)),
            dma((groups,)),
            dma((n, 1 + groups)),
            dma((n, 1 + groups)),
            dma((PIECES, 2)),
            dma((PIECES, nc - 1)),
            dma((PIECES, nc - 1)),
            dma((PIECES, nz - 1)),
            dma((PIECES, nz - 1)),
            dma((PIECES, nz - 1)),
            dma((PIECES, nz - 1)),
        ],
        compiler_params=pltpu.CompilerParams(
            collective_id=0, has_side_effects=True, vmem_limit_bytes=VMEM_BYTES
        ),
        name="layer",
    )(
        tile_rows[0], tile_cols[0], self_blocks[0], feats, adj, weight, proj_bias[None],
        cotangent[0],
    )
    return (hidden[None], weight_grad.astype(jnp.float32))


def solution(mesh):
    return jax.shard_map(
        functools.partial(per_device, mesh.shape["feat"], mesh.shape["grp"]),
        mesh=mesh,
        in_specs=(
            P("grp", None, "feat", None),
            P("grp", None, None, None),
            P("grp", None),
            P("grp", None),
            P("grp", None),
            P(),
            P(),
            P("grp", "feat", None),
        ),
        out_specs=(P("grp", "feat", None), P("feat", None)),
        check_vma=False,
    )
```

```python
import functools
import math

import jax
import jax.numpy as jnp
from jax import lax
from jax.experimental import pallas as pl
from jax.experimental.pallas import tpu as pltpu
from jax.sharding import PartitionSpec as P

MESH = pl.DeviceIdType.MESH
PIECES = 3
GROUP = 2
VMEM_BYTES = 60 * 1024 * 1024


def layer_kernel(
    n, nz, rows_ref, cols_ref, blocks_ref, feat_hbm, adj_hbm, w_hbm, bias_ref, cot_hbm,
    hid_hbm, grad_ref,
    feat, adj, w, cot, hidden, sendbuf, recvbuf, scan, last, comb_ref,
    pg, lhs, picked, mine, pair_out, pair_in, own, one_out, one_in, two_out, two_in, red,
    z_out, z_in, g_out, g_in,
    load_sem, hid_sem, send_sem, recv_sem,
    pair_sem, one_ssem, one_rsem, two_ssem, two_rsem, z_ssem, z_rsem, g_ssem, g_rsem,
):
    me = lax.axis_index("feat")
    mz = lax.axis_index("grp")
    nc = n // 2
    chip, core = me // 2, lax.rem(me, 2)
    sibling = chip * 2 + (1 - core)
    share, hid = grad_ref.shape
    piece = share // PIECES
    part = one_out.shape[3]
    parts = piece // part
    count = PIECES * parts
    side = one_out.shape[2]
    cw = hid // nz
    rows = sendbuf.shape[2]
    width = feat.shape[1]
    tiles = adj.shape[0]
    groups = rows // GROUP
    step_nodes = GROUP * 128
    step_cols = 256

    def chip_at(outer, inner):
        return lax.rem(chip // side + outer, side) * side + lax.rem(chip + inner, side)

    def z_at(i):
        return lax.rem(mz + i, nz)

    loads = [
        pltpu.make_async_copy(src, dst, load_sem.at[k])
        for k, (src, dst) in enumerate(
            [(feat_hbm, feat), (adj_hbm, adj), (w_hbm, w), (cot_hbm, cot)]
        )
    ]
    loads[0].start()

    barrier = pltpu.get_barrier_semaphore()

    def greet(i, carry):
        pl.semaphore_signal(
            barrier, inc=1, device_id={"feat": lax.rem(me + i, n)}, device_id_type=MESH
        )
        return carry

    lax.fori_loop(1, n, greet, 0)
    for i in range(1, nz):
        pl.semaphore_signal(barrier, inc=1, device_id={"grp": z_at(i)}, device_id_type=MESH)

    def fill_self(i, carry):
        peer = lax.rem(me + i, n)
        for r in range(rows):
            sendbuf[i, 0, r] = feat[blocks_ref[peer * rows + r]]
        return carry

    def self_copy(i, src):
        return pltpu.make_async_remote_copy(
            src_ref=sendbuf.at[i, 0],
            dst_ref=recvbuf.at[src, 0],
            send_sem=send_sem.at[i, 0],
            recv_sem=recv_sem.at[src, 0],
            device_id={"feat": lax.rem(me + i, n)},
            device_id_type=MESH,
        )

    def agg_copy(i, q, src):
        some = pl.ds(q * GROUP, GROUP)
        return pltpu.make_async_remote_copy(
            src_ref=sendbuf.at[i, 1, some],
            dst_ref=recvbuf.at[src, 1, some],
            send_sem=send_sem.at[i, 1 + q],
            recv_sem=recv_sem.at[src, 1 + q],
            device_id={"feat": lax.rem(me + i, n)},
            device_id_type=MESH,
        )

    def send_self(i, carry):
        fill_self(i, carry)
        self_copy(i, me).start()
        return carry

    loads[0].wait()
    for load in loads[1:]:
        load.start()
    fill_self(1, 0)
    pl.semaphore_wait(barrier, (n - 1) + (nz - 1))
    self_copy(1, me).start()
    lax.fori_loop(2, n, send_self, 0)
    for r in range(rows):
        recvbuf[me, 0, r] = feat[blocks_ref[me * rows + r]]

    loads[1].wait()

    def tile_terms(step, carry):
        for k in range(8):
            t = step * 8 + k
            scan[t] = lax.dot_general(
                feat[cols_ref[t]], adj[t], (((1,), (1,)), ((), ())),
                preferred_element_type=jnp.float32,
            )
        return carry

    lax.fori_loop(0, tiles // 8, tile_terms, 0)

    def running_sums(step, acc):
        for k in range(8):
            t = step * 8 + k
            same = rows_ref[t] == rows_ref[jnp.maximum(t - 1, 0)]
            acc = scan[t] + jnp.where(same, 1.0, 0.0) * acc
            scan[t] = acc
        return acc

    lax.fori_loop(0, tiles // 8, running_sums, jnp.zeros((width, 128), jnp.float32))

    def find_last(r, carry):
        at = jnp.int32(0)
        step = 1 << (tiles.bit_length() - 1)
        while step:
            there = at + step
            fits = (there < tiles) & (rows_ref[jnp.minimum(there, tiles - 1)] <= r)
            at = jnp.where(fits, there, at)
            step //= 2
        last[r] = at
        return carry

    lax.fori_loop(0, n * rows, find_last, 0)

    def send_group(q, carry):
        def send_agg(i, inner):
            peer = lax.rem(me + i, n)
            for k in range(GROUP):
                r = q * GROUP + k
                sendbuf[i, 1, r] = scan[last[peer * rows + r]].astype(jnp.bfloat16)
            agg_copy(i, q, me).start()
            return inner

        return lax.fori_loop(1, n, send_agg, carry)

    lax.fori_loop(0, groups, send_group, 0)
    for r in range(rows):
        recvbuf[me, 1, r] = scan[last[me * rows + r]].astype(jnp.bfloat16)

    loads[2].wait()
    loads[3].wait()

    def wait_self(i, carry):
        self_copy(i, lax.rem(me - i + n, n)).wait_recv()
        return carry

    lax.fori_loop(1, n, wait_self, 0)

    def hid_copy(q):
        at = pl.ds(pl.multiple_of(q * step_nodes, step_nodes), step_nodes)
        return pltpu.make_async_copy(hidden.at[at], hid_hbm.at[at], hid_sem.at[q])

    def forward(q, carry):
        def wait_agg(i, inner):
            agg_copy(i, q, lax.rem(me - i + n, n)).wait_recv()
            return inner

        lax.fori_loop(1, n, wait_agg, 0)
        for kind in range(2):
            base = kind * n * width
            for k in range(GROUP):
                r = q * GROUP + k
                lanes = pl.ds(pl.multiple_of(r * 128, 128), 128)
                if width % 16 == 0:
                    for src in range(n):
                        comb_ref[pl.ds(base + src * width, width), lanes] = recvbuf[src, kind, r]
                else:
                    whole = jnp.concatenate(
                        [recvbuf[src, kind, r].astype(jnp.float32) for src in range(n)], axis=0
                    )
                    comb_ref[pl.ds(base, n * width), lanes] = whole.astype(jnp.bfloat16)

        at = pl.ds(pl.multiple_of(q * step_nodes, step_nodes), step_nodes)
        lhs[...] = comb_ref[:, at].T

        def forward_columns(k, inner):
            some = pl.ds(pl.multiple_of(k * step_cols, step_cols), step_cols)
            pre = jnp.dot(lhs[...], w[:, some], preferred_element_type=jnp.float32)
            pre = pre + bias_ref[:, some]
            decay = jnp.exp(jnp.minimum(pre, 0.0))
            hidden[at, some] = jnp.where(pre > 0, pre, decay - 1.0).astype(jnp.bfloat16)
            pg[at, some] = (cot[at, some].astype(jnp.float32) * decay).astype(jnp.bfloat16)
            return inner

        lax.fori_loop(0, hid // step_cols, forward_columns, 0)
        hid_copy(q).start()
        return carry

    lax.fori_loop(0, groups, forward, 0)

    def terms(p, parity, out):
        for i in range(nc):
            owner = chip_at(i // side, i % side) * 2 + parity
            at = pl.multiple_of(owner * share + p * piece, piece)
            picked[i * piece:(i + 1) * piece] = comb_ref[pl.ds(at, piece), :]

        def some_columns(k, carry):
            some = pl.ds(pl.multiple_of(k * step_cols, step_cols), step_cols)
            out[:, some] = jnp.dot(
                picked[...], pg[:, some], preferred_element_type=jnp.float32
            )
            return carry

        lax.fori_loop(0, hid // step_cols, some_columns, 0)

    def pair_copy(p):
        return pltpu.make_async_remote_copy(
            src_ref=pair_out.at[p], dst_ref=pair_in.at[p],
            send_sem=pair_sem.at[p, 0], recv_sem=pair_sem.at[p, 1],
            device_id={"feat": sibling}, device_id_type=MESH,
        )

    def offsets(c, phase, i):
        return (0, i) if (c + phase) % 2 == 0 else (i, 0)

    def block_rows(c, outer, inner):
        return pl.ds((outer * side + inner) * piece + (c % parts) * part, part)

    def one_copy(c, i):
        return pltpu.make_async_remote_copy(
            src_ref=one_out.at[c, i - 1], dst_ref=one_in.at[c, i - 1],
            send_sem=one_ssem.at[c, i - 1], recv_sem=one_rsem.at[c, i - 1],
            device_id={"feat": chip_at(*offsets(c, 0, i)) * 2 + core}, device_id_type=MESH,
        )

    def two_copy(c, i):
        return pltpu.make_async_remote_copy(
            src_ref=two_out.at[c, i - 1], dst_ref=two_in.at[c, i - 1],
            send_sem=two_ssem.at[c, i - 1], recv_sem=two_rsem.at[c, i - 1],
            device_id={"feat": chip_at(*offsets(c, 1, i)) * 2 + core}, device_id_type=MESH,
        )

    def z_copy(c, i):
        return pltpu.make_async_remote_copy(
            src_ref=z_out.at[c, i - 1], dst_ref=z_in.at[c, i - 1],
            send_sem=z_ssem.at[c, i - 1], recv_sem=z_rsem.at[c, i - 1],
            device_id={"grp": z_at(i)}, device_id_type=MESH,
        )

    def g_copy(c, i):
        return pltpu.make_async_remote_copy(
            src_ref=g_out.at[c], dst_ref=g_in.at[c, i - 1],
            send_sem=g_ssem.at[c, i - 1], recv_sem=g_rsem.at[c, i - 1],
            device_id={"grp": z_at(i)}, device_id_type=MESH,
        )

    def columns(z):
        return pl.ds(pl.multiple_of(z * cw, cw), cw)

    def pair_stage(p):
        terms(p, 1 - core, pair_out.at[p])
        pair_copy(p).start()

    def one_stage(p):
        terms(p, core, mine.at[p])
        pair_copy(p).wait_recv()
        for c in range(p * parts, (p + 1) * parts):
            for i in range(1, side):
                for j in range(side):
                    first, second = offsets(c, 0, i), offsets(c, 1, j)
                    at = block_rows(c, first[0] + second[0], first[1] + second[1])
                    one_out[c, i - 1, j] = (mine[p, at] + pair_in[p, at]).astype(jnp.bfloat16)
                one_copy(c, i).start()

    def two_stage(c):
        p = c // parts
        for i in range(1, side):
            one_copy(c, i).wait_recv()
        for j in list(range(1, side)) + [0]:
            at = block_rows(c, *offsets(c, 1, j))
            total = mine[p, at] + pair_in[p, at]
            for i in range(1, side):
                total = total + one_in[c, i - 1, j].astype(jnp.float32)
            if j:
                two_out[c, j - 1] = total.astype(jnp.bfloat16)
                two_copy(c, j).start()
            else:
                own[c] = total

    def z_stage(c):
        total = own[c]
        for i in range(1, side):
            two_copy(c, i).wait_recv()
            total = total + two_in[c, i - 1].astype(jnp.float32)
        red[c] = total
        for i in range(1, nz):
            z_out[c, i - 1] = red[c, :, columns(z_at(i))].astype(jnp.bfloat16)
            z_copy(c, i).start()

    def g_stage(c):
        total = red[c, :, columns(mz)]
        for i in range(1, nz):
            z_copy(c, i).wait_recv()
            total = total + z_in[c, i - 1].astype(jnp.float32)
        g_out[c] = total.astype(jnp.bfloat16)
        for i in range(1, nz):
            g_copy(c, i).start()
        grad_ref[pl.ds(c * part, part), columns(mz)] = g_out[c].astype(jnp.float32)

    def last_stage(c):
        for i in range(1, nz):
            g_copy(c, i).wait_recv()
            grad_ref[pl.ds(c * part, part), columns(lax.rem(mz - i + nz, nz))] = (
                g_in[c, i - 1].astype(jnp.float32)
            )

    pair_stage(0)
    pair_stage(1)
    one_stage(0)
    pair_stage(2)
    one_stage(1)
    two_stage(0)
    one_stage(2)
    for c in range(1, count + 2):
        if c < count:
            two_stage(c)
        if c - 1 < count:
            z_stage(c - 1)
        g_stage(c - 2) if c >= 2 else None
    for c in range(count):
        last_stage(c)
    for p in range(PIECES):
        pair_copy(p).wait_send()
    for c in range(count):
        for i in range(1, side):
            one_copy(c, i).wait_send()
            two_copy(c, i).wait_send()
        for i in range(1, nz):
            z_copy(c, i).wait_send()
            g_copy(c, i).wait_send()

    def wait_out(i, carry):
        self_copy(i, me).wait_send()
        for q in range(groups):
            agg_copy(i, q, me).wait_send()
        return carry

    lax.fori_loop(1, n, wait_out, 0)
    for q in range(groups):
        hid_copy(q).wait()


def per_device(
    n, nz,
    features, adj_tiles, tile_rows, tile_cols, self_blocks, weight, proj_bias, cotangent,
):
    feats, adj = features[0], adj_tiles[0]
    width, side = feats.shape[1], feats.shape[2]
    tiles = adj.shape[0]
    block_count = self_blocks.shape[1]
    rows = block_count // n
    depth, hid = weight.shape
    nodes = rows * side
    share = depth // n
    piece = share // PIECES
    nc = n // 2
    grid = math.isqrt(nc)
    part = 32 if piece % 32 == 0 else piece
    count = share // part
    cw = hid // nz
    groups = rows // GROUP
    step_nodes = GROUP * side

    smem = pl.BlockSpec(memory_space=pltpu.SMEM)
    vmem = pl.BlockSpec(memory_space=pltpu.VMEM)
    anywhere = pl.BlockSpec(memory_space=pl.ANY)
    dma = pltpu.SemaphoreType.DMA
    hidden, weight_grad = pl.pallas_call(
        functools.partial(layer_kernel, n, nz),
        out_shape=(
            jax.ShapeDtypeStruct((nodes, hid), jnp.bfloat16),
            jax.ShapeDtypeStruct((share, hid), jnp.float32),
        ),
        in_specs=[smem] * 3 + [anywhere] * 3 + [vmem, anywhere],
        out_specs=(anywhere, vmem),
        scratch_shapes=[
            pltpu.VMEM(feats.shape, jnp.bfloat16),
            pltpu.VMEM(adj.shape, jnp.bfloat16),
            pltpu.VMEM(weight.shape, jnp.bfloat16),
            pltpu.VMEM((nodes, hid), jnp.bfloat16),
            pltpu.VMEM((nodes, hid), jnp.bfloat16),
            pltpu.VMEM((n, 2, rows, width, side), jnp.bfloat16),
            pltpu.VMEM((n, 2, rows, width, side), jnp.bfloat16),
            pltpu.VMEM((tiles, width, side), jnp.float32),
            pltpu.SMEM((block_count,), jnp.int32),
            pltpu.VMEM((depth, nodes), jnp.bfloat16),
            pltpu.VMEM((nodes, hid), jnp.bfloat16),
            pltpu.VMEM((step_nodes, depth), jnp.bfloat16),
            pltpu.VMEM((nc * piece, nodes), jnp.bfloat16),
            pltpu.VMEM((PIECES, nc * piece, hid), jnp.float32),
            pltpu.VMEM((PIECES, nc * piece, hid), jnp.float32),
            pltpu.VMEM((PIECES, nc * piece, hid), jnp.float32),
            pltpu.VMEM((count, part, hid), jnp.float32),
            pltpu.VMEM((count, grid - 1, grid, part, hid), jnp.bfloat16),
            pltpu.VMEM((count, grid - 1, grid, part, hid), jnp.bfloat16),
            pltpu.VMEM((count, grid - 1, part, hid), jnp.bfloat16),
            pltpu.VMEM((count, grid - 1, part, hid), jnp.bfloat16),
            pltpu.VMEM((count, part, hid), jnp.float32),
            pltpu.VMEM((count, nz - 1, part, cw), jnp.bfloat16),
            pltpu.VMEM((count, nz - 1, part, cw), jnp.bfloat16),
            pltpu.VMEM((count, part, cw), jnp.bfloat16),
            pltpu.VMEM((count, nz - 1, part, cw), jnp.bfloat16),
            dma((4,)),
            dma((groups,)),
            dma((n, 1 + groups)),
            dma((n, 1 + groups)),
            dma((PIECES, 2)),
            dma((count, grid - 1)),
            dma((count, grid - 1)),
            dma((count, grid - 1)),
            dma((count, grid - 1)),
            dma((count, nz - 1)),
            dma((count, nz - 1)),
            dma((count, nz - 1)),
            dma((count, nz - 1)),
        ],
        compiler_params=pltpu.CompilerParams(
            collective_id=0, has_side_effects=True, vmem_limit_bytes=VMEM_BYTES
        ),
        name="layer",
    )(
        tile_rows[0], tile_cols[0], self_blocks[0], feats, adj, weight, proj_bias[None],
        cotangent[0],
    )
    return (hidden[None], weight_grad)


def solution(mesh):
    return jax.shard_map(
        functools.partial(per_device, mesh.shape["feat"], mesh.shape["grp"]),
        mesh=mesh,
        in_specs=(
            P("grp", None, "feat", None),
            P("grp", None, None, None),
            P("grp", None),
            P("grp", None),
            P("grp", None),
            P(),
            P(),
            P("grp", "feat", None),
        ),
        out_specs=(P("grp", "feat", None), P("feat", None)),
        check_vma=False,
    )
```

```python
import functools

import jax
import jax.numpy as jnp
from jax import lax
from jax.experimental import pallas as pl
from jax.experimental.pallas import tpu as pltpu
from jax.sharding import PartitionSpec as P

MESH = pl.DeviceIdType.MESH
PIECES = 3
GROUP = 2
VMEM_BYTES = 60 * 1024 * 1024


def layer_kernel(
    n, nz, rows_ref, cols_ref, blocks_ref, feat_hbm, adj_hbm, w_hbm, bias_ref, cot_hbm,
    hid_hbm, grad_ref,
    feat, adj, w, cot, hidden, sendbuf, recvbuf, scan, last, comb_ref,
    pg, pre, lhs, picked, mine, pair_out, pair_in, own, chip_out, chip_in, red,
    z_out, z_in, g_out, g_in,
    load_sem, hid_sem, send_sem, recv_sem,
    pair_sem, chip_ssem, chip_rsem, z_ssem, z_rsem, g_ssem, g_rsem,
):
    me = lax.axis_index("feat")
    mz = lax.axis_index("grp")
    nc = n // 2
    chip, core = me // 2, lax.rem(me, 2)
    sibling = chip * 2 + (1 - core)
    share, hid = grad_ref.shape
    piece = share // PIECES
    cw = hid // nz
    rows = sendbuf.shape[2]
    width = feat.shape[1]
    tiles = adj.shape[0]
    groups = rows // GROUP
    step_nodes = GROUP * 128
    step_cols = 256

    def chip_at(i):
        return lax.rem(chip + i, nc) * 2 + core

    def z_at(i):
        return lax.rem(mz + i, nz)

    loads = [
        pltpu.make_async_copy(src, dst, load_sem.at[k])
        for k, (src, dst) in enumerate(
            [(feat_hbm, feat), (adj_hbm, adj), (w_hbm, w), (cot_hbm, cot)]
        )
    ]
    loads[0].start()

    barrier = pltpu.get_barrier_semaphore()

    def greet(i, carry):
        pl.semaphore_signal(
            barrier, inc=1, device_id={"feat": lax.rem(me + i, n)}, device_id_type=MESH
        )
        return carry

    lax.fori_loop(1, n, greet, 0)
    for i in range(1, nz):
        pl.semaphore_signal(barrier, inc=1, device_id={"grp": z_at(i)}, device_id_type=MESH)

    def fill_self(i, carry):
        peer = lax.rem(me + i, n)
        for r in range(rows):
            sendbuf[i, 0, r] = feat[blocks_ref[peer * rows + r]]
        return carry

    def self_copy(i, src):
        return pltpu.make_async_remote_copy(
            src_ref=sendbuf.at[i, 0],
            dst_ref=recvbuf.at[src, 0],
            send_sem=send_sem.at[i, 0],
            recv_sem=recv_sem.at[src, 0],
            device_id={"feat": lax.rem(me + i, n)},
            device_id_type=MESH,
        )

    def agg_copy(i, q, src):
        some = pl.ds(q * GROUP, GROUP)
        return pltpu.make_async_remote_copy(
            src_ref=sendbuf.at[i, 1, some],
            dst_ref=recvbuf.at[src, 1, some],
            send_sem=send_sem.at[i, 1 + q],
            recv_sem=recv_sem.at[src, 1 + q],
            device_id={"feat": lax.rem(me + i, n)},
            device_id_type=MESH,
        )

    def send_self(i, carry):
        fill_self(i, carry)
        self_copy(i, me).start()
        return carry

    def find_last(r, carry):
        at = jnp.int32(0)
        step = 1 << (tiles.bit_length() - 1)
        while step:
            there = at + step
            fits = (there < tiles) & (rows_ref[jnp.minimum(there, tiles - 1)] <= r)
            at = jnp.where(fits, there, at)
            step //= 2
        last[r] = at
        return carry

    lax.fori_loop(0, n * rows, find_last, 0)
    loads[0].wait()
    for load in loads[1:]:
        load.start()
    fill_self(1, 0)
    pl.semaphore_wait(barrier, (n - 1) + (nz - 1))
    self_copy(1, me).start()
    lax.fori_loop(2, n, send_self, 0)
    for r in range(rows):
        recvbuf[me, 0, r] = feat[blocks_ref[me * rows + r]]

    loads[1].wait()

    def tile_terms(step, carry):
        for k in range(8):
            t = step * 8 + k
            scan[t] = lax.dot_general(
                feat[cols_ref[t]], adj[t], (((1,), (1,)), ((), ())),
                preferred_element_type=jnp.float32,
            )
        return carry

    lax.fori_loop(0, tiles // 8, tile_terms, 0)

    def running_sums(step, acc):
        for k in range(8):
            t = step * 8 + k
            same = rows_ref[t] == rows_ref[jnp.maximum(t - 1, 0)]
            acc = scan[t] + jnp.where(same, 1.0, 0.0) * acc
            scan[t] = acc
        return acc

    lax.fori_loop(0, tiles // 8, running_sums, jnp.zeros((width, 128), jnp.float32))

    def send_group(q, carry):
        def send_agg(i, inner):
            peer = lax.rem(me + i, n)
            for k in range(GROUP):
                r = q * GROUP + k
                sendbuf[i, 1, r] = scan[last[peer * rows + r]].astype(jnp.bfloat16)
            agg_copy(i, q, me).start()
            return inner

        return lax.fori_loop(1, n, send_agg, carry)

    lax.fori_loop(0, groups, send_group, 0)
    for r in range(rows):
        recvbuf[me, 1, r] = scan[last[me * rows + r]].astype(jnp.bfloat16)

    loads[2].wait()
    loads[3].wait()

    def wait_self(i, carry):
        self_copy(i, lax.rem(me - i + n, n)).wait_recv()
        return carry

    lax.fori_loop(1, n, wait_self, 0)

    def hid_copy(q):
        at = pl.ds(pl.multiple_of(q * step_nodes, step_nodes), step_nodes)
        return pltpu.make_async_copy(hidden.at[at], hid_hbm.at[at], hid_sem.at[q])

    half = n * width

    def place(q, kind):
        base = kind * half
        for k in range(GROUP):
            r = q * GROUP + k
            lanes = pl.ds(pl.multiple_of(r * 128, 128), 128)
            if width % 16 == 0:
                for src in range(n):
                    comb_ref[pl.ds(base + src * width, width), lanes] = recvbuf[src, kind, r]
            else:
                whole = jnp.concatenate(
                    [recvbuf[src, kind, r].astype(jnp.float32) for src in range(n)], axis=0
                )
                comb_ref[pl.ds(base, half), lanes] = whole.astype(jnp.bfloat16)
        at = pl.ds(pl.multiple_of(q * step_nodes, step_nodes), step_nodes)
        lhs[...] = comb_ref[pl.ds(base, half), at].T
        return at

    def forward_self(q, carry):
        at = place(q, 0)

        def self_columns(k, inner):
            some = pl.ds(pl.multiple_of(k * step_cols, step_cols), step_cols)
            pre[at, some] = bias_ref[:, some] + jnp.dot(
                lhs[...], w[:half, some], preferred_element_type=jnp.float32
            )
            return inner

        return lax.fori_loop(0, hid // step_cols, self_columns, carry)

    lax.fori_loop(0, groups, forward_self, 0)

    def forward(q, carry):
        def wait_agg(i, inner):
            agg_copy(i, q, lax.rem(me - i + n, n)).wait_recv()
            return inner

        lax.fori_loop(1, n, wait_agg, 0)
        at = place(q, 1)

        def forward_columns(k, inner):
            some = pl.ds(pl.multiple_of(k * step_cols, step_cols), step_cols)
            value = pre[at, some] + jnp.dot(
                lhs[...], w[half:, some], preferred_element_type=jnp.float32
            )
            decay = jnp.exp(jnp.minimum(value, 0.0))
            hidden[at, some] = jnp.where(value > 0, value, decay - 1.0).astype(jnp.bfloat16)
            pg[at, some] = (cot[at, some].astype(jnp.float32) * decay).astype(jnp.bfloat16)
            return inner

        lax.fori_loop(0, hid // step_cols, forward_columns, 0)
        hid_copy(q).start()
        return carry

    lax.fori_loop(0, groups, forward, 0)

    def terms(p, parity, out):
        for i in range(nc):
            owner = lax.rem(chip + i, nc) * 2 + parity
            at = pl.multiple_of(owner * share + p * piece, piece)
            picked[i * piece:(i + 1) * piece] = comb_ref[pl.ds(at, piece), :]

        def some_columns(k, carry):
            some = pl.ds(pl.multiple_of(k * step_cols, step_cols), step_cols)
            out[:, some] = jnp.dot(
                picked[...], pg[:, some], preferred_element_type=jnp.float32
            ).astype(out.dtype)
            return carry

        lax.fori_loop(0, hid // step_cols, some_columns, 0)

    def pair_copy(p):
        return pltpu.make_async_remote_copy(
            src_ref=pair_out.at[p], dst_ref=pair_in.at[p],
            send_sem=pair_sem.at[p, 0], recv_sem=pair_sem.at[p, 1],
            device_id={"feat": sibling}, device_id_type=MESH,
        )

    def chip_copy(p, i):
        return pltpu.make_async_remote_copy(
            src_ref=chip_out.at[p, i - 1], dst_ref=chip_in.at[p, i - 1],
            send_sem=chip_ssem.at[p, i - 1], recv_sem=chip_rsem.at[p, i - 1],
            device_id={"feat": chip_at(i)}, device_id_type=MESH,
        )

    def z_copy(p, i):
        return pltpu.make_async_remote_copy(
            src_ref=z_out.at[p, i - 1], dst_ref=z_in.at[p, i - 1],
            send_sem=z_ssem.at[p, i - 1], recv_sem=z_rsem.at[p, i - 1],
            device_id={"grp": z_at(i)}, device_id_type=MESH,
        )

    def g_copy(p, i):
        return pltpu.make_async_remote_copy(
            src_ref=g_out.at[p], dst_ref=g_in.at[p, i - 1],
            send_sem=g_ssem.at[p, i - 1], recv_sem=g_rsem.at[p, i - 1],
            device_id={"grp": z_at(i)}, device_id_type=MESH,
        )

    def columns(z):
        return pl.ds(pl.multiple_of(z * cw, cw), cw)

    def pair_stage(p):
        terms(p, 1 - core, pair_out.at[p])
        pair_copy(p).start()

    def chip_stage(p):
        terms(p, core, mine)
        pair_copy(p).wait_recv()
        own[p] = mine[:piece] + pair_in[p, :piece].astype(jnp.float32)
        for i in range(1, nc):
            part = pl.ds(i * piece, piece)
            chip_out[p, i - 1] = (mine[part] + pair_in[p, part].astype(jnp.float32)).astype(jnp.bfloat16)
            chip_copy(p, i).start()

    def z_stage(p):
        total = own[p]
        for i in range(1, nc):
            chip_copy(p, i).wait_recv()
            total = total + chip_in[p, i - 1].astype(jnp.float32)
        red[p] = total
        for i in range(1, nz):
            z_out[p, i - 1] = red[p, :, columns(z_at(i))].astype(jnp.bfloat16)
            z_copy(p, i).start()

    def g_stage(p):
        total = red[p, :, columns(mz)]
        for i in range(1, nz):
            z_copy(p, i).wait_recv()
            total = total + z_in[p, i - 1].astype(jnp.float32)
        g_out[p] = total.astype(jnp.bfloat16)
        for i in range(1, nz):
            g_copy(p, i).start()
        grad_ref[pl.ds(p * piece, piece), columns(mz)] = g_out[p].astype(jnp.float32)

    def last_stage(p):
        for i in range(1, nz):
            g_copy(p, i).wait_recv()
            grad_ref[pl.ds(p * piece, piece), columns(lax.rem(mz - i + nz, nz))] = (
                g_in[p, i - 1].astype(jnp.float32)
            )

    pair_stage(0)
    pair_stage(1)
    chip_stage(0)
    pair_stage(2)
    chip_stage(1)
    chip_stage(2)
    z_stage(0)
    z_stage(1)
    g_stage(0)
    z_stage(2)
    g_stage(1)
    g_stage(2)
    for p in range(PIECES):
        last_stage(p)
    for p in range(PIECES):
        pair_copy(p).wait_send()
        for i in range(1, nc):
            chip_copy(p, i).wait_send()
        for i in range(1, nz):
            z_copy(p, i).wait_send()
            g_copy(p, i).wait_send()

    def wait_out(i, carry):
        self_copy(i, me).wait_send()
        for q in range(groups):
            agg_copy(i, q, me).wait_send()
        return carry

    lax.fori_loop(1, n, wait_out, 0)
    for q in range(groups):
        hid_copy(q).wait()


def per_device(
    n, nz,
    features, adj_tiles, tile_rows, tile_cols, self_blocks, weight, proj_bias, cotangent,
):
    feats, adj = features[0], adj_tiles[0]
    width, side = feats.shape[1], feats.shape[2]
    tiles = adj.shape[0]
    block_count = self_blocks.shape[1]
    rows = block_count // n
    depth, hid = weight.shape
    nodes = rows * side
    share = depth // n
    piece = share // PIECES
    nc = n // 2
    cw = hid // nz
    groups = rows // GROUP
    step_nodes = GROUP * side

    smem = pl.BlockSpec(memory_space=pltpu.SMEM)
    vmem = pl.BlockSpec(memory_space=pltpu.VMEM)
    anywhere = pl.BlockSpec(memory_space=pl.ANY)
    dma = pltpu.SemaphoreType.DMA
    hidden, weight_grad = pl.pallas_call(
        functools.partial(layer_kernel, n, nz),
        out_shape=(
            jax.ShapeDtypeStruct((nodes, hid), jnp.bfloat16),
            jax.ShapeDtypeStruct((share, hid), jnp.float32),
        ),
        in_specs=[smem] * 3 + [anywhere] * 3 + [vmem, anywhere],
        out_specs=(anywhere, vmem),
        scratch_shapes=[
            pltpu.VMEM(feats.shape, jnp.bfloat16),
            pltpu.VMEM(adj.shape, jnp.bfloat16),
            pltpu.VMEM(weight.shape, jnp.bfloat16),
            pltpu.VMEM((nodes, hid), jnp.bfloat16),
            pltpu.VMEM((nodes, hid), jnp.bfloat16),
            pltpu.VMEM((n, 2, rows, width, side), jnp.bfloat16),
            pltpu.VMEM((n, 2, rows, width, side), jnp.bfloat16),
            pltpu.VMEM((tiles, width, side), jnp.float32),
            pltpu.SMEM((block_count,), jnp.int32),
            pltpu.VMEM((depth, nodes), jnp.bfloat16),
            pltpu.VMEM((nodes, hid), jnp.bfloat16),
            pltpu.VMEM((nodes, hid), jnp.float32),
            pltpu.VMEM((step_nodes, depth // 2), jnp.bfloat16),
            pltpu.VMEM((nc * piece, nodes), jnp.bfloat16),
            pltpu.VMEM((nc * piece, hid), jnp.float32),
            pltpu.VMEM((PIECES, nc * piece, hid), jnp.bfloat16),
            pltpu.VMEM((PIECES, nc * piece, hid), jnp.bfloat16),
            pltpu.VMEM((PIECES, piece, hid), jnp.float32),
            pltpu.VMEM((PIECES, nc - 1, piece, hid), jnp.bfloat16),
            pltpu.VMEM((PIECES, nc - 1, piece, hid), jnp.bfloat16),
            pltpu.VMEM((PIECES, piece, hid), jnp.float32),
            pltpu.VMEM((PIECES, nz - 1, piece, cw), jnp.bfloat16),
            pltpu.VMEM((PIECES, nz - 1, piece, cw), jnp.bfloat16),
            pltpu.VMEM((PIECES, piece, cw), jnp.bfloat16),
            pltpu.VMEM((PIECES, nz - 1, piece, cw), jnp.bfloat16),
            dma((4,)),
            dma((groups,)),
            dma((n, 1 + groups)),
            dma((n, 1 + groups)),
            dma((PIECES, 2)),
            dma((PIECES, nc - 1)),
            dma((PIECES, nc - 1)),
            dma((PIECES, nz - 1)),
            dma((PIECES, nz - 1)),
            dma((PIECES, nz - 1)),
            dma((PIECES, nz - 1)),
        ],
        compiler_params=pltpu.CompilerParams(
            collective_id=0, has_side_effects=True, vmem_limit_bytes=VMEM_BYTES
        ),
        name="layer",
    )(
        tile_rows[0], tile_cols[0], self_blocks[0], feats, adj, weight, proj_bias[None],
        cotangent[0],
    )
    return (hidden[None], weight_grad)


def solution(mesh):
    return jax.shard_map(
        functools.partial(per_device, mesh.shape["feat"], mesh.shape["grp"]),
        mesh=mesh,
        in_specs=(
            P("grp", None, "feat", None),
            P("grp", None, None, None),
            P("grp", None),
            P("grp", None),
            P("grp", None),
            P(),
            P(),
            P("grp", "feat", None),
        ),
        out_specs=(P("grp", "feat", None), P("feat", None)),
        check_vma=False,
    )
```

```python
import functools

import jax
import jax.numpy as jnp
from jax import lax
from jax.experimental import pallas as pl
from jax.experimental.pallas import tpu as pltpu
from jax.sharding import PartitionSpec as P

MESH = pl.DeviceIdType.MESH
PIECES = 3
GROUP = 2
VMEM_BYTES = 60 * 1024 * 1024


def layer_kernel(
    n, nz, rows_ref, cols_ref, blocks_ref, feat_hbm, adj_hbm, w_hbm, bias_ref, cot_hbm,
    hid_hbm, grad_ref,
    feat, adj, w, cot, hidden, sendbuf, recvbuf, scan, last, comb_ref,
    pg, pre, lhs, picked, acc, mine, pair_out, pair_in, own, chip_out, chip_in, red,
    z_out, z_in, g_out, g_in,
    load_sem, hid_sem, send_sem, recv_sem,
    pair_sem, chip_ssem, chip_rsem, z_ssem, z_rsem, g_ssem, g_rsem,
):
    me = lax.axis_index("feat")
    mz = lax.axis_index("grp")
    nc = n // 2
    chip, core = me // 2, lax.rem(me, 2)
    sibling = chip * 2 + (1 - core)
    share, hid = grad_ref.shape
    piece = share // PIECES
    cw = hid // nz
    rows = sendbuf.shape[2]
    width = feat.shape[1]
    tiles = adj.shape[0]
    groups = rows // GROUP
    step_nodes = GROUP * 128
    step_cols = 256

    def chip_at(i):
        return lax.rem(chip + i, nc) * 2 + core

    def z_at(i):
        return lax.rem(mz + i, nz)

    loads = [
        pltpu.make_async_copy(src, dst, load_sem.at[k])
        for k, (src, dst) in enumerate(
            [(feat_hbm, feat), (adj_hbm, adj), (w_hbm, w), (cot_hbm, cot)]
        )
    ]
    loads[0].start()

    barrier = pltpu.get_barrier_semaphore()

    def greet(i, carry):
        pl.semaphore_signal(
            barrier, inc=1, device_id={"feat": lax.rem(me + i, n)}, device_id_type=MESH
        )
        return carry

    lax.fori_loop(1, n, greet, 0)
    for i in range(1, nz):
        pl.semaphore_signal(barrier, inc=1, device_id={"grp": z_at(i)}, device_id_type=MESH)

    def fill_self(i, carry):
        peer = lax.rem(me + i, n)
        for r in range(rows):
            sendbuf[i, 0, r] = feat[blocks_ref[peer * rows + r]]
        return carry

    def self_copy(i, src):
        return pltpu.make_async_remote_copy(
            src_ref=sendbuf.at[i, 0],
            dst_ref=recvbuf.at[src, 0],
            send_sem=send_sem.at[i, 0],
            recv_sem=recv_sem.at[src, 0],
            device_id={"feat": lax.rem(me + i, n)},
            device_id_type=MESH,
        )

    def agg_copy(i, q, src):
        some = pl.ds(q * GROUP, GROUP)
        return pltpu.make_async_remote_copy(
            src_ref=sendbuf.at[i, 1, some],
            dst_ref=recvbuf.at[src, 1, some],
            send_sem=send_sem.at[i, 1 + q],
            recv_sem=recv_sem.at[src, 1 + q],
            device_id={"feat": lax.rem(me + i, n)},
            device_id_type=MESH,
        )

    def send_self(i, carry):
        fill_self(i, carry)
        self_copy(i, me).start()
        return carry

    def find_last(r, carry):
        at = jnp.int32(0)
        step = 1 << (tiles.bit_length() - 1)
        while step:
            there = at + step
            fits = (there < tiles) & (rows_ref[jnp.minimum(there, tiles - 1)] <= r)
            at = jnp.where(fits, there, at)
            step //= 2
        last[r] = at
        return carry

    lax.fori_loop(0, n * rows, find_last, 0)
    loads[0].wait()
    for load in loads[1:]:
        load.start()
    fill_self(1, 0)
    pl.semaphore_wait(barrier, (n - 1) + (nz - 1))
    self_copy(1, me).start()
    lax.fori_loop(2, n, send_self, 0)
    for r in range(rows):
        recvbuf[me, 0, r] = feat[blocks_ref[me * rows + r]]

    loads[1].wait()

    def tile_terms(step, carry):
        for k in range(8):
            t = step * 8 + k
            scan[t] = lax.dot_general(
                feat[cols_ref[t]], adj[t], (((1,), (1,)), ((), ())),
                preferred_element_type=jnp.float32,
            )
        return carry

    lax.fori_loop(0, tiles // 8, tile_terms, 0)

    def running_sums(step, acc):
        for k in range(8):
            t = step * 8 + k
            same = rows_ref[t] == rows_ref[jnp.maximum(t - 1, 0)]
            acc = scan[t] + jnp.where(same, 1.0, 0.0) * acc
            scan[t] = acc
        return acc

    lax.fori_loop(0, tiles // 8, running_sums, jnp.zeros((width, 128), jnp.float32))

    def send_group(q, carry):
        def send_agg(i, inner):
            peer = lax.rem(me + i, n)
            for k in range(GROUP):
                r = q * GROUP + k
                sendbuf[i, 1, r] = scan[last[peer * rows + r]].astype(jnp.bfloat16)
            agg_copy(i, q, me).start()
            return inner

        return lax.fori_loop(1, n, send_agg, carry)

    lax.fori_loop(0, groups, send_group, 0)
    for r in range(rows):
        recvbuf[me, 1, r] = scan[last[me * rows + r]].astype(jnp.bfloat16)

    loads[2].wait()
    loads[3].wait()

    def wait_self(i, carry):
        self_copy(i, lax.rem(me - i + n, n)).wait_recv()
        return carry

    lax.fori_loop(1, n, wait_self, 0)

    def hid_copy(q):
        at = pl.ds(pl.multiple_of(q * step_nodes, step_nodes), step_nodes)
        return pltpu.make_async_copy(hidden.at[at], hid_hbm.at[at], hid_sem.at[q])

    half = n * width

    def place(q, kind):
        base = kind * half
        for k in range(GROUP):
            r = q * GROUP + k
            lanes = pl.ds(pl.multiple_of(r * 128, 128), 128)
            if width % 16 == 0:
                for src in range(n):
                    comb_ref[pl.ds(base + src * width, width), lanes] = recvbuf[src, kind, r]
            else:
                whole = jnp.concatenate(
                    [recvbuf[src, kind, r].astype(jnp.float32) for src in range(n)], axis=0
                )
                comb_ref[pl.ds(base, half), lanes] = whole.astype(jnp.bfloat16)
        at = pl.ds(pl.multiple_of(q * step_nodes, step_nodes), step_nodes)
        lhs[...] = comb_ref[pl.ds(base, half), at].T
        return at

    def forward_self(q, carry):
        at = place(q, 0)

        def self_columns(k, inner):
            some = pl.ds(pl.multiple_of(k * step_cols, step_cols), step_cols)
            pre[at, some] = bias_ref[:, some] + jnp.dot(
                lhs[...], w[:half, some], preferred_element_type=jnp.float32
            )
            return inner

        return lax.fori_loop(0, hid // step_cols, self_columns, carry)

    lax.fori_loop(0, groups, forward_self, 0)

    def forward(q, carry):
        def wait_agg(i, inner):
            agg_copy(i, q, lax.rem(me - i + n, n)).wait_recv()
            return inner

        lax.fori_loop(1, n, wait_agg, 0)
        at = place(q, 1)

        def forward_columns(k, inner):
            some = pl.ds(pl.multiple_of(k * step_cols, step_cols), step_cols)
            value = pre[at, some] + jnp.dot(
                lhs[...], w[half:, some], preferred_element_type=jnp.float32
            )
            decay = jnp.exp(jnp.minimum(value, 0.0))
            hidden[at, some] = jnp.where(value > 0, value, decay - 1.0).astype(jnp.bfloat16)
            pg[at, some] = (cot[at, some].astype(jnp.float32) * decay).astype(jnp.bfloat16)
            return inner

        lax.fori_loop(0, hid // step_cols, forward_columns, 0)
        hid_copy(q).start()
        return carry

    def pick(p, parity, at):
        for i in range(nc):
            owner = lax.rem(chip + i, nc) * 2 + parity
            place_at = pl.multiple_of(owner * share + p * piece, piece)
            picked[i * piece:(i + 1) * piece] = comb_ref[pl.ds(place_at, piece), at]

    def group_nodes(q):
        return pl.ds(pl.multiple_of(q * step_nodes, step_nodes), step_nodes)

    def gather_terms(q, first):
        at = group_nodes(q)

        def one_part(k, carry):
            p, whose = k // 2, lax.rem(k, 2)
            pick(p, jnp.where(whose == 1, core, 1 - core), at)

            def some_columns(h, inner):
                some = pl.ds(pl.multiple_of(h * step_cols, step_cols), step_cols)
                term = jnp.dot(picked[...], pg[at, some], preferred_element_type=jnp.float32)
                if first:
                    acc[k, :, some] = term
                else:
                    acc[k, :, some] += term
                return inner

            return lax.fori_loop(0, hid // step_cols, some_columns, carry)

        lax.fori_loop(0, 2 * PIECES, one_part, 0)

    def terms(p, whose, out):
        at = group_nodes(groups - 1)
        pick(p, core if whose else 1 - core, at)

        def some_columns(h, carry):
            some = pl.ds(pl.multiple_of(h * step_cols, step_cols), step_cols)
            term = jnp.dot(picked[...], pg[at, some], preferred_element_type=jnp.float32)
            out[:, some] = (acc[2 * p + whose, :, some] + term).astype(out.dtype)
            return carry

        lax.fori_loop(0, hid // step_cols, some_columns, 0)

    forward(0, 0)
    gather_terms(0, True)

    def forward_and_terms(q, carry):
        forward(q, carry)
        gather_terms(q, False)
        return carry

    lax.fori_loop(1, groups - 1, forward_and_terms, 0)
    forward(groups - 1, 0)

    def pair_copy(p):
        return pltpu.make_async_remote_copy(
            src_ref=pair_out.at[p], dst_ref=pair_in.at[p],
            send_sem=pair_sem.at[p, 0], recv_sem=pair_sem.at[p, 1],
            device_id={"feat": sibling}, device_id_type=MESH,
        )

    def chip_copy(p, i):
        return pltpu.make_async_remote_copy(
            src_ref=chip_out.at[p, i - 1], dst_ref=chip_in.at[p, i - 1],
            send_sem=chip_ssem.at[p, i - 1], recv_sem=chip_rsem.at[p, i - 1],
            device_id={"feat": chip_at(i)}, device_id_type=MESH,
        )

    def z_copy(p, i):
        return pltpu.make_async_remote_copy(
            src_ref=z_out.at[p, i - 1], dst_ref=z_in.at[p, i - 1],
            send_sem=z_ssem.at[p, i - 1], recv_sem=z_rsem.at[p, i - 1],
            device_id={"grp": z_at(i)}, device_id_type=MESH,
        )

    def g_copy(p, i):
        return pltpu.make_async_remote_copy(
            src_ref=g_out.at[p], dst_ref=g_in.at[p, i - 1],
            send_sem=g_ssem.at[p, i - 1], recv_sem=g_rsem.at[p, i - 1],
            device_id={"grp": z_at(i)}, device_id_type=MESH,
        )

    def columns(z):
        return pl.ds(pl.multiple_of(z * cw, cw), cw)

    def pair_stage(p):
        terms(p, 0, pair_out.at[p])
        pair_copy(p).start()

    def chip_stage(p):
        terms(p, 1, mine)
        pair_copy(p).wait_recv()
        own[p] = mine[:piece] + pair_in[p, :piece].astype(jnp.float32)
        for i in range(1, nc):
            part = pl.ds(i * piece, piece)
            chip_out[p, i - 1] = (mine[part] + pair_in[p, part].astype(jnp.float32)).astype(jnp.bfloat16)
            chip_copy(p, i).start()

    def z_stage(p):
        total = own[p]
        for i in range(1, nc):
            chip_copy(p, i).wait_recv()
            total = total + chip_in[p, i - 1].astype(jnp.float32)
        red[p] = total
        for i in range(1, nz):
            z_out[p, i - 1] = red[p, :, columns(z_at(i))].astype(jnp.bfloat16)
            z_copy(p, i).start()

    def g_stage(p):
        total = red[p, :, columns(mz)]
        for i in range(1, nz):
            z_copy(p, i).wait_recv()
            total = total + z_in[p, i - 1].astype(jnp.float32)
        g_out[p] = total.astype(jnp.bfloat16)
        for i in range(1, nz):
            g_copy(p, i).start()
        grad_ref[pl.ds(p * piece, piece), columns(mz)] = g_out[p].astype(jnp.float32)

    def last_stage(p):
        for i in range(1, nz):
            g_copy(p, i).wait_recv()
            grad_ref[pl.ds(p * piece, piece), columns(lax.rem(mz - i + nz, nz))] = (
                g_in[p, i - 1].astype(jnp.float32)
            )

    pair_stage(0)
    pair_stage(1)
    chip_stage(0)
    pair_stage(2)
    chip_stage(1)
    chip_stage(2)
    z_stage(0)
    z_stage(1)
    g_stage(0)
    z_stage(2)
    g_stage(1)
    g_stage(2)
    for p in range(PIECES):
        last_stage(p)
    for p in range(PIECES):
        pair_copy(p).wait_send()
        for i in range(1, nc):
            chip_copy(p, i).wait_send()
        for i in range(1, nz):
            z_copy(p, i).wait_send()
            g_copy(p, i).wait_send()

    def wait_out(i, carry):
        self_copy(i, me).wait_send()
        for q in range(groups):
            agg_copy(i, q, me).wait_send()
        return carry

    lax.fori_loop(1, n, wait_out, 0)
    for q in range(groups):
        hid_copy(q).wait()


def per_device(
    n, nz,
    features, adj_tiles, tile_rows, tile_cols, self_blocks, weight, proj_bias, cotangent,
):
    feats, adj = features[0], adj_tiles[0]
    width, side = feats.shape[1], feats.shape[2]
    tiles = adj.shape[0]
    block_count = self_blocks.shape[1]
    rows = block_count // n
    depth, hid = weight.shape
    nodes = rows * side
    share = depth // n
    piece = share // PIECES
    nc = n // 2
    cw = hid // nz
    groups = rows // GROUP
    step_nodes = GROUP * side

    smem = pl.BlockSpec(memory_space=pltpu.SMEM)
    vmem = pl.BlockSpec(memory_space=pltpu.VMEM)
    anywhere = pl.BlockSpec(memory_space=pl.ANY)
    dma = pltpu.SemaphoreType.DMA
    hidden, weight_grad = pl.pallas_call(
        functools.partial(layer_kernel, n, nz),
        out_shape=(
            jax.ShapeDtypeStruct((nodes, hid), jnp.bfloat16),
            jax.ShapeDtypeStruct((share, hid), jnp.float32),
        ),
        in_specs=[smem] * 3 + [anywhere] * 3 + [vmem, anywhere],
        out_specs=(anywhere, vmem),
        scratch_shapes=[
            pltpu.VMEM(feats.shape, jnp.bfloat16),
            pltpu.VMEM(adj.shape, jnp.bfloat16),
            pltpu.VMEM(weight.shape, jnp.bfloat16),
            pltpu.VMEM((nodes, hid), jnp.bfloat16),
            pltpu.VMEM((nodes, hid), jnp.bfloat16),
            pltpu.VMEM((n, 2, rows, width, side), jnp.bfloat16),
            pltpu.VMEM((n, 2, rows, width, side), jnp.bfloat16),
            pltpu.VMEM((tiles, width, side), jnp.float32),
            pltpu.SMEM((block_count,), jnp.int32),
            pltpu.VMEM((depth, nodes), jnp.bfloat16),
            pltpu.VMEM((nodes, hid), jnp.bfloat16),
            pltpu.VMEM((nodes, hid), jnp.float32),
            pltpu.VMEM((step_nodes, depth // 2), jnp.bfloat16),
            pltpu.VMEM((nc * piece, step_nodes), jnp.bfloat16),
            pltpu.VMEM((2 * PIECES, nc * piece, hid), jnp.float32),
            pltpu.VMEM((nc * piece, hid), jnp.float32),
            pltpu.VMEM((PIECES, nc * piece, hid), jnp.bfloat16),
            pltpu.VMEM((PIECES, nc * piece, hid), jnp.bfloat16),
            pltpu.VMEM((PIECES, piece, hid), jnp.float32),
            pltpu.VMEM((PIECES, nc - 1, piece, hid), jnp.bfloat16),
            pltpu.VMEM((PIECES, nc - 1, piece, hid), jnp.bfloat16),
            pltpu.VMEM((PIECES, piece, hid), jnp.float32),
            pltpu.VMEM((PIECES, nz - 1, piece, cw), jnp.bfloat16),
            pltpu.VMEM((PIECES, nz - 1, piece, cw), jnp.bfloat16),
            pltpu.VMEM((PIECES, piece, cw), jnp.bfloat16),
            pltpu.VMEM((PIECES, nz - 1, piece, cw), jnp.bfloat16),
            dma((4,)),
            dma((groups,)),
            dma((n, 1 + groups)),
            dma((n, 1 + groups)),
            dma((PIECES, 2)),
            dma((PIECES, nc - 1)),
            dma((PIECES, nc - 1)),
            dma((PIECES, nz - 1)),
            dma((PIECES, nz - 1)),
            dma((PIECES, nz - 1)),
            dma((PIECES, nz - 1)),
        ],
        compiler_params=pltpu.CompilerParams(
            collective_id=0, has_side_effects=True, vmem_limit_bytes=VMEM_BYTES
        ),
        name="layer",
    )(
        tile_rows[0], tile_cols[0], self_blocks[0], feats, adj, weight, proj_bias[None],
        cotangent[0],
    )
    return (hidden[None], weight_grad)


def solution(mesh):
    return jax.shard_map(
        functools.partial(per_device, mesh.shape["feat"], mesh.shape["grp"]),
        mesh=mesh,
        in_specs=(
            P("grp", None, "feat", None),
            P("grp", None, None, None),
            P("grp", None),
            P("grp", None),
            P("grp", None),
            P(),
            P(),
            P("grp", "feat", None),
        ),
        out_specs=(P("grp", "feat", None), P("feat", None)),
        check_vma=False,
    )
```

```python
import functools

import jax
import jax.numpy as jnp
from jax import lax
from jax.experimental import pallas as pl
from jax.experimental.pallas import tpu as pltpu
from jax.sharding import PartitionSpec as P

MESH = pl.DeviceIdType.MESH
PIECES = 3
GROUP = 2
VMEM_BYTES = 60 * 1024 * 1024


def layer_kernel(
    n, nz, rows_ref, cols_ref, blocks_ref, feat_hbm, adj_hbm, w_hbm, bias_ref, cot_hbm,
    hid_hbm, grad_ref,
    feat, adj, w, cot, hidden, sendbuf, recvbuf, scan, last, comb_ref,
    pg, pre, lhs, picked, mine, pair_out, pair_in, own, chip_out, chip_in, red,
    z_out, z_in, g_out, g_in,
    load_sem, hid_sem, send_sem, recv_sem,
    pair_sem, chip_ssem, chip_rsem, z_ssem, z_rsem, g_ssem, g_rsem,
):
    me = lax.axis_index("feat")
    mz = lax.axis_index("grp")
    nc = n // 2
    chip, core = me // 2, lax.rem(me, 2)
    sibling = chip * 2 + (1 - core)
    share, hid = grad_ref.shape
    piece = share // PIECES
    cw = hid // nz
    rows = sendbuf.shape[2]
    width = feat.shape[1]
    tiles = adj.shape[0]
    groups = rows // GROUP
    step_nodes = GROUP * 128
    step_cols = hid // 2

    def chip_at(i):
        return lax.rem(chip + i, nc) * 2 + core

    def z_at(i):
        return lax.rem(mz + i, nz)

    loads = [
        pltpu.make_async_copy(src, dst, load_sem.at[k])
        for k, (src, dst) in enumerate(
            [(feat_hbm, feat), (adj_hbm, adj), (w_hbm, w), (cot_hbm, cot)]
        )
    ]
    loads[0].start()

    barrier = pltpu.get_barrier_semaphore()

    def greet(i, carry):
        pl.semaphore_signal(
            barrier, inc=1, device_id={"feat": lax.rem(me + i, n)}, device_id_type=MESH
        )
        return carry

    lax.fori_loop(1, n, greet, 0)
    for i in range(1, nz):
        pl.semaphore_signal(barrier, inc=1, device_id={"grp": z_at(i)}, device_id_type=MESH)

    def fill_self(i, carry):
        peer = lax.rem(me + i, n)
        for r in range(rows):
            sendbuf[i, 0, r] = feat[blocks_ref[peer * rows + r]]
        return carry

    def self_copy(i, src):
        return pltpu.make_async_remote_copy(
            src_ref=sendbuf.at[i, 0],
            dst_ref=recvbuf.at[src, 0],
            send_sem=send_sem.at[i, 0],
            recv_sem=recv_sem.at[src, 0],
            device_id={"feat": lax.rem(me + i, n)},
            device_id_type=MESH,
        )

    def agg_copy(i, q, src):
        some = pl.ds(q * GROUP, GROUP)
        return pltpu.make_async_remote_copy(
            src_ref=sendbuf.at[i, 1, some],
            dst_ref=recvbuf.at[src, 1, some],
            send_sem=send_sem.at[i, 1 + q],
            recv_sem=recv_sem.at[src, 1 + q],
            device_id={"feat": lax.rem(me + i, n)},
            device_id_type=MESH,
        )

    def send_self(i, carry):
        fill_self(i, carry)
        self_copy(i, me).start()
        return carry

    def find_last(r, carry):
        at = jnp.int32(0)
        step = 1 << (tiles.bit_length() - 1)
        while step:
            there = at + step
            fits = (there < tiles) & (rows_ref[jnp.minimum(there, tiles - 1)] <= r)
            at = jnp.where(fits, there, at)
            step //= 2
        last[r] = at
        return carry

    lax.fori_loop(0, n * rows, find_last, 0)
    loads[0].wait()
    for load in loads[1:]:
        load.start()
    fill_self(1, 0)
    pl.semaphore_wait(barrier, (n - 1) + (nz - 1))
    self_copy(1, me).start()
    lax.fori_loop(2, n, send_self, 0)
    for r in range(rows):
        recvbuf[me, 0, r] = feat[blocks_ref[me * rows + r]]

    loads[1].wait()

    def tile_terms(step, carry):
        for k in range(16):
            t = step * 16 + k
            scan[t] = lax.dot_general(
                feat[cols_ref[t]], adj[t], (((1,), (1,)), ((), ())),
                preferred_element_type=jnp.float32,
            )
        return carry

    lax.fori_loop(0, tiles // 16, tile_terms, 0)

    def running_sums(step, acc):
        for k in range(8):
            t = step * 8 + k
            same = rows_ref[t] == rows_ref[jnp.maximum(t - 1, 0)]
            acc = scan[t] + jnp.where(same, 1.0, 0.0) * acc
            scan[t] = acc
        return acc

    lax.fori_loop(0, tiles // 8, running_sums, jnp.zeros((width, 128), jnp.float32))

    def send_group(q, carry):
        def send_agg(i, inner):
            peer = lax.rem(me + i, n)
            for k in range(GROUP):
                r = q * GROUP + k
                sendbuf[i, 1, r] = scan[last[peer * rows + r]].astype(jnp.bfloat16)
            agg_copy(i, q, me).start()
            return inner

        return lax.fori_loop(1, n, send_agg, carry)

    lax.fori_loop(0, groups, send_group, 0)
    for r in range(rows):
        recvbuf[me, 1, r] = scan[last[me * rows + r]].astype(jnp.bfloat16)

    loads[2].wait()
    loads[3].wait()

    def wait_self(i, carry):
        self_copy(i, lax.rem(me - i + n, n)).wait_recv()
        return carry

    lax.fori_loop(1, n, wait_self, 0)

    def hid_copy(q):
        at = pl.ds(pl.multiple_of(q * step_nodes, step_nodes), step_nodes)
        return pltpu.make_async_copy(hidden.at[at], hid_hbm.at[at], hid_sem.at[q])

    half = n * width

    def place(q, kind):
        base = kind * half
        for k in range(GROUP):
            r = q * GROUP + k
            lanes = pl.ds(pl.multiple_of(r * 128, 128), 128)
            if width % 16 == 0:
                for src in range(n):
                    comb_ref[pl.ds(base + src * width, width), lanes] = recvbuf[src, kind, r]
            else:
                whole = jnp.concatenate(
                    [recvbuf[src, kind, r].astype(jnp.float32) for src in range(n)], axis=0
                )
                comb_ref[pl.ds(base, half), lanes] = whole.astype(jnp.bfloat16)
        at = pl.ds(pl.multiple_of(q * step_nodes, step_nodes), step_nodes)
        lhs[...] = comb_ref[pl.ds(base, half), at].T
        return at

    def forward_self(q, carry):
        at = place(q, 0)

        def self_columns(k, inner):
            some = pl.ds(pl.multiple_of(k * step_cols, step_cols), step_cols)
            pre[at, some] = bias_ref[:, some] + jnp.dot(
                lhs[...], w[:half, some], preferred_element_type=jnp.float32
            )
            return inner

        return lax.fori_loop(0, hid // step_cols, self_columns, carry)

    lax.fori_loop(0, groups, forward_self, 0)

    def forward(q, carry):
        def wait_agg(i, inner):
            agg_copy(i, q, lax.rem(me - i + n, n)).wait_recv()
            return inner

        lax.fori_loop(1, n, wait_agg, 0)
        at = place(q, 1)

        def forward_columns(k, inner):
            some = pl.ds(pl.multiple_of(k * step_cols, step_cols), step_cols)
            value = pre[at, some] + jnp.dot(
                lhs[...], w[half:, some], preferred_element_type=jnp.float32
            )
            decay = jnp.exp(jnp.minimum(value, 0.0))
            hidden[at, some] = jnp.where(value > 0, value, decay - 1.0).astype(jnp.bfloat16)
            pg[at, some] = (cot[at, some].astype(jnp.float32) * decay).astype(jnp.bfloat16)
            return inner

        lax.fori_loop(0, hid // step_cols, forward_columns, 0)
        hid_copy(q).start()
        return carry

    lax.fori_loop(0, groups, forward, 0)

    def terms(p, parity, out):
        for i in range(nc):
            owner = lax.rem(chip + i, nc) * 2 + parity
            at = pl.multiple_of(owner * share + p * piece, piece)
            picked[i * piece:(i + 1) * piece] = comb_ref[pl.ds(at, piece), :]

        out[...] = jnp.dot(
            picked[...], pg[...], preferred_element_type=jnp.float32
        ).astype(out.dtype)

    def pair_copy(p):
        return pltpu.make_async_remote_copy(
            src_ref=pair_out.at[p], dst_ref=pair_in.at[p],
            send_sem=pair_sem.at[p, 0], recv_sem=pair_sem.at[p, 1],
            device_id={"feat": sibling}, device_id_type=MESH,
        )

    def chip_copy(p, i):
        return pltpu.make_async_remote_copy(
            src_ref=chip_out.at[p, i - 1], dst_ref=chip_in.at[p, i - 1],
            send_sem=chip_ssem.at[p, i - 1], recv_sem=chip_rsem.at[p, i - 1],
            device_id={"feat": chip_at(i)}, device_id_type=MESH,
        )

    def z_copy(p, i):
        return pltpu.make_async_remote_copy(
            src_ref=z_out.at[p, i - 1], dst_ref=z_in.at[p, i - 1],
            send_sem=z_ssem.at[p, i - 1], recv_sem=z_rsem.at[p, i - 1],
            device_id={"grp": z_at(i)}, device_id_type=MESH,
        )

    def g_copy(p, i):
        return pltpu.make_async_remote_copy(
            src_ref=g_out.at[p], dst_ref=g_in.at[p, i - 1],
            send_sem=g_ssem.at[p, i - 1], recv_sem=g_rsem.at[p, i - 1],
            device_id={"grp": z_at(i)}, device_id_type=MESH,
        )

    def columns(z):
        return pl.ds(pl.multiple_of(z * cw, cw), cw)

    def pair_stage(p):
        terms(p, 1 - core, pair_out.at[p])
        pair_copy(p).start()

    def chip_stage(p):
        terms(p, core, mine)
        pair_copy(p).wait_recv()
        own[p] = mine[:piece] + pair_in[p, :piece].astype(jnp.float32)
        for i in range(1, nc):
            part = pl.ds(i * piece, piece)
            chip_out[p, i - 1] = (mine[part] + pair_in[p, part].astype(jnp.float32)).astype(jnp.bfloat16)
            chip_copy(p, i).start()

    def z_stage(p):
        total = own[p]
        for i in range(1, nc):
            chip_copy(p, i).wait_recv()
            total = total + chip_in[p, i - 1].astype(jnp.float32)
        red[p] = total
        for i in range(1, nz):
            z_out[p, i - 1] = red[p, :, columns(z_at(i))].astype(jnp.bfloat16)
            z_copy(p, i).start()

    def g_stage(p):
        total = red[p, :, columns(mz)]
        for i in range(1, nz):
            z_copy(p, i).wait_recv()
            total = total + z_in[p, i - 1].astype(jnp.float32)
        g_out[p] = total.astype(jnp.bfloat16)
        for i in range(1, nz):
            g_copy(p, i).start()
        grad_ref[pl.ds(p * piece, piece), columns(mz)] = g_out[p].astype(jnp.float32)

    def last_stage(p):
        for i in range(1, nz):
            g_copy(p, i).wait_recv()
            grad_ref[pl.ds(p * piece, piece), columns(lax.rem(mz - i + nz, nz))] = (
                g_in[p, i - 1].astype(jnp.float32)
            )

    pair_stage(0)
    pair_stage(1)
    chip_stage(0)
    pair_stage(2)
    chip_stage(1)
    chip_stage(2)
    z_stage(0)
    z_stage(1)
    g_stage(0)
    z_stage(2)
    g_stage(1)
    g_stage(2)
    for p in range(PIECES):
        last_stage(p)
    for p in range(PIECES):
        pair_copy(p).wait_send()
        for i in range(1, nc):
            chip_copy(p, i).wait_send()
        for i in range(1, nz):
            z_copy(p, i).wait_send()
            g_copy(p, i).wait_send()

    def wait_out(i, carry):
        self_copy(i, me).wait_send()
        for q in range(groups):
            agg_copy(i, q, me).wait_send()
        return carry

    lax.fori_loop(1, n, wait_out, 0)
    for q in range(groups):
        hid_copy(q).wait()


def per_device(
    n, nz,
    features, adj_tiles, tile_rows, tile_cols, self_blocks, weight, proj_bias, cotangent,
):
    feats, adj = features[0], adj_tiles[0]
    width, side = feats.shape[1], feats.shape[2]
    tiles = adj.shape[0]
    block_count = self_blocks.shape[1]
    rows = block_count // n
    depth, hid = weight.shape
    nodes = rows * side
    share = depth // n
    piece = share // PIECES
    nc = n // 2
    cw = hid // nz
    groups = rows // GROUP
    step_nodes = GROUP * side

    smem = pl.BlockSpec(memory_space=pltpu.SMEM)
    vmem = pl.BlockSpec(memory_space=pltpu.VMEM)
    anywhere = pl.BlockSpec(memory_space=pl.ANY)
    dma = pltpu.SemaphoreType.DMA
    hidden, weight_grad = pl.pallas_call(
        functools.partial(layer_kernel, n, nz),
        out_shape=(
            jax.ShapeDtypeStruct((nodes, hid), jnp.bfloat16),
            jax.ShapeDtypeStruct((share, hid), jnp.float32),
        ),
        in_specs=[smem] * 3 + [anywhere] * 3 + [vmem, anywhere],
        out_specs=(anywhere, vmem),
        scratch_shapes=[
            pltpu.VMEM(feats.shape, jnp.bfloat16),
            pltpu.VMEM(adj.shape, jnp.bfloat16),
            pltpu.VMEM(weight.shape, jnp.bfloat16),
            pltpu.VMEM((nodes, hid), jnp.bfloat16),
            pltpu.VMEM((nodes, hid), jnp.bfloat16),
            pltpu.VMEM((n, 2, rows, width, side), jnp.bfloat16),
            pltpu.VMEM((n, 2, rows, width, side), jnp.bfloat16),
            pltpu.VMEM((tiles, width, side), jnp.float32),
            pltpu.SMEM((block_count,), jnp.int32),
            pltpu.VMEM((depth, nodes), jnp.bfloat16),
            pltpu.VMEM((nodes, hid), jnp.bfloat16),
            pltpu.VMEM((nodes, hid), jnp.float32),
            pltpu.VMEM((step_nodes, depth // 2), jnp.bfloat16),
            pltpu.VMEM((nc * piece, nodes), jnp.bfloat16),
            pltpu.VMEM((nc * piece, hid), jnp.float32),
            pltpu.VMEM((PIECES, nc * piece, hid), jnp.bfloat16),
            pltpu.VMEM((PIECES, nc * piece, hid), jnp.bfloat16),
            pltpu.VMEM((PIECES, piece, hid), jnp.float32),
            pltpu.VMEM((PIECES, nc - 1, piece, hid), jnp.bfloat16),
            pltpu.VMEM((PIECES, nc - 1, piece, hid), jnp.bfloat16),
            pltpu.VMEM((PIECES, piece, hid), jnp.float32),
            pltpu.VMEM((PIECES, nz - 1, piece, cw), jnp.bfloat16),
            pltpu.VMEM((PIECES, nz - 1, piece, cw), jnp.bfloat16),
            pltpu.VMEM((PIECES, piece, cw), jnp.bfloat16),
            pltpu.VMEM((PIECES, nz - 1, piece, cw), jnp.bfloat16),
            dma((4,)),
            dma((groups,)),
            dma((n, 1 + groups)),
            dma((n, 1 + groups)),
            dma((PIECES, 2)),
            dma((PIECES, nc - 1)),
            dma((PIECES, nc - 1)),
            dma((PIECES, nz - 1)),
            dma((PIECES, nz - 1)),
            dma((PIECES, nz - 1)),
            dma((PIECES, nz - 1)),
        ],
        compiler_params=pltpu.CompilerParams(
            collective_id=0, has_side_effects=True, vmem_limit_bytes=VMEM_BYTES
        ),
        name="layer",
    )(
        tile_rows[0], tile_cols[0], self_blocks[0], feats, adj, weight, proj_bias[None],
        cotangent[0],
    )
    return (hidden[None], weight_grad)


def solution(mesh):
    return jax.shard_map(
        functools.partial(per_device, mesh.shape["feat"], mesh.shape["grp"]),
        mesh=mesh,
        in_specs=(
            P("grp", None, "feat", None),
            P("grp", None, None, None),
            P("grp", None),
            P("grp", None),
            P("grp", None),
            P(),
            P(),
            P("grp", "feat", None),
        ),
        out_specs=(P("grp", "feat", None), P("feat", None)),
        check_vma=False,
    )
```

```python
import functools

import jax
import jax.numpy as jnp
from jax import lax
from jax.experimental import pallas as pl
from jax.experimental.pallas import tpu as pltpu
from jax.sharding import PartitionSpec as P

MESH = pl.DeviceIdType.MESH
GROUP = 2
VMEM_BYTES = 60 * 1024 * 1024


def pieces_of(share):
    return 4 if share % 64 == 0 else 3


def layer_kernel(
    n, nz, rows_ref, cols_ref, blocks_ref, feat_hbm, adj_hbm, w_hbm, bias_ref, cot_hbm,
    hid_hbm, grad_ref,
    feat, adj, w, cot, hidden, sendbuf, recvbuf, scan, last, comb_ref,
    pg, pre, lhs, picked, mine, pair_out, pair_in, own, chip_out, chip_in, red,
    z_out, z_in, g_out, g_in,
    load_sem, hid_sem, send_sem, recv_sem,
    pair_sem, chip_ssem, chip_rsem, z_ssem, z_rsem, g_ssem, g_rsem,
):
    me = lax.axis_index("feat")
    mz = lax.axis_index("grp")
    nc = n // 2
    chip, core = me // 2, lax.rem(me, 2)
    sibling = chip * 2 + (1 - core)
    share, hid = grad_ref.shape
    pieces = pieces_of(share)
    piece = share // pieces
    cw = hid // nz
    rows = sendbuf.shape[2]
    width = feat.shape[1]
    tiles = adj.shape[0]
    groups = rows // GROUP
    step_nodes = GROUP * 128
    step_cols = hid // 2

    def chip_at(i):
        return lax.rem(chip + i, nc) * 2 + core

    def z_at(i):
        return lax.rem(mz + i, nz)

    loads = [
        pltpu.make_async_copy(src, dst, load_sem.at[k])
        for k, (src, dst) in enumerate(
            [(feat_hbm, feat), (adj_hbm, adj), (w_hbm, w), (cot_hbm, cot)]
        )
    ]
    loads[0].start()

    barrier = pltpu.get_barrier_semaphore()

    def greet(i, carry):
        pl.semaphore_signal(
            barrier, inc=1, device_id={"feat": lax.rem(me + i, n)}, device_id_type=MESH
        )
        return carry

    lax.fori_loop(1, n, greet, 0)
    for i in range(1, nz):
        pl.semaphore_signal(barrier, inc=1, device_id={"grp": z_at(i)}, device_id_type=MESH)

    def fill_self(i, carry):
        peer = lax.rem(me + i, n)
        for r in range(rows):
            sendbuf[i, 0, r] = feat[blocks_ref[peer * rows + r]]
        return carry

    def self_copy(i, src):
        return pltpu.make_async_remote_copy(
            src_ref=sendbuf.at[i, 0],
            dst_ref=recvbuf.at[src, 0],
            send_sem=send_sem.at[i, 0],
            recv_sem=recv_sem.at[src, 0],
            device_id={"feat": lax.rem(me + i, n)},
            device_id_type=MESH,
        )

    def agg_copy(i, q, src):
        some = pl.ds(q * GROUP, GROUP)
        return pltpu.make_async_remote_copy(
            src_ref=sendbuf.at[i, 1, some],
            dst_ref=recvbuf.at[src, 1, some],
            send_sem=send_sem.at[i, 1 + q],
            recv_sem=recv_sem.at[src, 1 + q],
            device_id={"feat": lax.rem(me + i, n)},
            device_id_type=MESH,
        )

    def send_self(i, carry):
        fill_self(i, carry)
        self_copy(i, me).start()
        return carry

    def find_last(r, carry):
        at = jnp.int32(0)
        step = 1 << (tiles.bit_length() - 1)
        while step:
            there = at + step
            fits = (there < tiles) & (rows_ref[jnp.minimum(there, tiles - 1)] <= r)
            at = jnp.where(fits, there, at)
            step //= 2
        last[r] = at
        return carry

    lax.fori_loop(0, n * rows, find_last, 0)
    loads[0].wait()
    for load in loads[1:]:
        load.start()
    fill_self(1, 0)
    pl.semaphore_wait(barrier, (n - 1) + (nz - 1))
    self_copy(1, me).start()
    lax.fori_loop(2, n, send_self, 0)
    for r in range(rows):
        recvbuf[me, 0, r] = feat[blocks_ref[me * rows + r]]

    loads[1].wait()

    def tile_terms(step, carry):
        for k in range(16):
            t = step * 16 + k
            scan[t] = lax.dot_general(
                feat[cols_ref[t]], adj[t], (((1,), (1,)), ((), ())),
                preferred_element_type=jnp.float32,
            )
        return carry

    lax.fori_loop(0, tiles // 16, tile_terms, 0)

    def running_sums(step, acc):
        for k in range(8):
            t = step * 8 + k
            same = rows_ref[t] == rows_ref[jnp.maximum(t - 1, 0)]
            acc = scan[t] + jnp.where(same, 1.0, 0.0) * acc
            scan[t] = acc
        return acc

    lax.fori_loop(0, tiles // 8, running_sums, jnp.zeros((width, 128), jnp.float32))

    def send_group(q, carry):
        def send_agg(i, inner):
            peer = lax.rem(me + i, n)
            for k in range(GROUP):
                r = q * GROUP + k
                sendbuf[i, 1, r] = scan[last[peer * rows + r]].astype(jnp.bfloat16)
            agg_copy(i, q, me).start()
            return inner

        return lax.fori_loop(1, n, send_agg, carry)

    lax.fori_loop(0, groups, send_group, 0)
    for r in range(rows):
        recvbuf[me, 1, r] = scan[last[me * rows + r]].astype(jnp.bfloat16)

    loads[2].wait()
    loads[3].wait()

    def wait_self(i, carry):
        self_copy(i, lax.rem(me - i + n, n)).wait_recv()
        return carry

    lax.fori_loop(1, n, wait_self, 0)

    def hid_copy(q):
        at = pl.ds(pl.multiple_of(q * step_nodes, step_nodes), step_nodes)
        return pltpu.make_async_copy(hidden.at[at], hid_hbm.at[at], hid_sem.at[q])

    half = n * width

    def place(q, kind):
        base = kind * half
        for k in range(GROUP):
            r = q * GROUP + k
            lanes = pl.ds(pl.multiple_of(r * 128, 128), 128)
            if width % 16 == 0:
                for src in range(n):
                    comb_ref[pl.ds(base + src * width, width), lanes] = recvbuf[src, kind, r]
            else:
                whole = jnp.concatenate(
                    [recvbuf[src, kind, r].astype(jnp.float32) for src in range(n)], axis=0
                )
                comb_ref[pl.ds(base, half), lanes] = whole.astype(jnp.bfloat16)
        at = pl.ds(pl.multiple_of(q * step_nodes, step_nodes), step_nodes)
        lhs[...] = comb_ref[pl.ds(base, half), at].T
        return at

    def forward_self(q, carry):
        at = place(q, 0)

        def self_columns(k, inner):
            some = pl.ds(pl.multiple_of(k * step_cols, step_cols), step_cols)
            pre[at, some] = bias_ref[:, some] + jnp.dot(
                lhs[...], w[:half, some], preferred_element_type=jnp.float32
            )
            return inner

        return lax.fori_loop(0, hid // step_cols, self_columns, carry)

    lax.fori_loop(0, groups, forward_self, 0)

    def forward(q, carry):
        def wait_agg(i, inner):
            agg_copy(i, q, lax.rem(me - i + n, n)).wait_recv()
            return inner

        lax.fori_loop(1, n, wait_agg, 0)
        at = place(q, 1)

        def forward_columns(k, inner):
            some = pl.ds(pl.multiple_of(k * step_cols, step_cols), step_cols)
            value = pre[at, some] + jnp.dot(
                lhs[...], w[half:, some], preferred_element_type=jnp.float32
            )
            decay = jnp.exp(jnp.minimum(value, 0.0))
            hidden[at, some] = jnp.where(value > 0, value, decay - 1.0).astype(jnp.bfloat16)
            pg[at, some] = (cot[at, some].astype(jnp.float32) * decay).astype(jnp.bfloat16)
            return inner

        lax.fori_loop(0, hid // step_cols, forward_columns, 0)
        hid_copy(q).start()
        return carry

    lax.fori_loop(0, groups, forward, 0)

    def terms(p, parity, out):
        for i in range(nc):
            owner = lax.rem(chip + i, nc) * 2 + parity
            at = pl.multiple_of(owner * share + p * piece, piece)
            picked[i * piece:(i + 1) * piece] = comb_ref[pl.ds(at, piece), :]

        out[...] = jnp.dot(
            picked[...], pg[...], preferred_element_type=jnp.float32
        ).astype(out.dtype)

    def pair_copy(p):
        return pltpu.make_async_remote_copy(
            src_ref=pair_out.at[p], dst_ref=pair_in.at[p],
            send_sem=pair_sem.at[p, 0], recv_sem=pair_sem.at[p, 1],
            device_id={"feat": sibling}, device_id_type=MESH,
        )

    def chip_copy(p, i):
        return pltpu.make_async_remote_copy(
            src_ref=chip_out.at[p, i - 1], dst_ref=chip_in.at[p, i - 1],
            send_sem=chip_ssem.at[p, i - 1], recv_sem=chip_rsem.at[p, i - 1],
            device_id={"feat": chip_at(i)}, device_id_type=MESH,
        )

    def z_copy(p, i):
        return pltpu.make_async_remote_copy(
            src_ref=z_out.at[p, i - 1], dst_ref=z_in.at[p, i - 1],
            send_sem=z_ssem.at[p, i - 1], recv_sem=z_rsem.at[p, i - 1],
            device_id={"grp": z_at(i)}, device_id_type=MESH,
        )

    def g_copy(p, i):
        return pltpu.make_async_remote_copy(
            src_ref=g_out.at[p], dst_ref=g_in.at[p, i - 1],
            send_sem=g_ssem.at[p, i - 1], recv_sem=g_rsem.at[p, i - 1],
            device_id={"grp": z_at(i)}, device_id_type=MESH,
        )

    def columns(z):
        return pl.ds(pl.multiple_of(z * cw, cw), cw)

    def pair_stage(p):
        terms(p, 1 - core, pair_out.at[p])
        pair_copy(p).start()

    def chip_stage(p):
        terms(p, core, mine)
        pair_copy(p).wait_recv()
        own[p] = mine[:piece] + pair_in[p, :piece].astype(jnp.float32)
        for i in range(1, nc):
            part = pl.ds(i * piece, piece)
            chip_out[p, i - 1] = (mine[part] + pair_in[p, part].astype(jnp.float32)).astype(jnp.bfloat16)
            chip_copy(p, i).start()

    def z_stage(p):
        total = own[p]
        for i in range(1, nc):
            chip_copy(p, i).wait_recv()
            total = total + chip_in[p, i - 1].astype(jnp.float32)
        red[p] = total
        for i in range(1, nz):
            z_out[p, i - 1] = red[p, :, columns(z_at(i))].astype(jnp.bfloat16)
            z_copy(p, i).start()

    def g_stage(p):
        total = red[p, :, columns(mz)]
        for i in range(1, nz):
            z_copy(p, i).wait_recv()
            total = total + z_in[p, i - 1].astype(jnp.float32)
        g_out[p] = total.astype(jnp.bfloat16)
        for i in range(1, nz):
            g_copy(p, i).start()
        grad_ref[pl.ds(p * piece, piece), columns(mz)] = g_out[p].astype(jnp.float32)

    def last_stage(p):
        for i in range(1, nz):
            g_copy(p, i).wait_recv()
            grad_ref[pl.ds(p * piece, piece), columns(lax.rem(mz - i + nz, nz))] = (
                g_in[p, i - 1].astype(jnp.float32)
            )

    pair_stage(0)
    for p in range(pieces):
        if p + 1 < pieces:
            pair_stage(p + 1)
        chip_stage(p)
    for p in range(pieces):
        z_stage(p)
        if p:
            g_stage(p - 1)
    g_stage(pieces - 1)
    for p in range(pieces):
        last_stage(p)
    for p in range(pieces):
        pair_copy(p).wait_send()
        for i in range(1, nc):
            chip_copy(p, i).wait_send()
        for i in range(1, nz):
            z_copy(p, i).wait_send()
            g_copy(p, i).wait_send()

    def wait_out(i, carry):
        self_copy(i, me).wait_send()
        for q in range(groups):
            agg_copy(i, q, me).wait_send()
        return carry

    lax.fori_loop(1, n, wait_out, 0)
    for q in range(groups):
        hid_copy(q).wait()


def per_device(
    n, nz,
    features, adj_tiles, tile_rows, tile_cols, self_blocks, weight, proj_bias, cotangent,
):
    feats, adj = features[0], adj_tiles[0]
    width, side = feats.shape[1], feats.shape[2]
    tiles = adj.shape[0]
    block_count = self_blocks.shape[1]
    rows = block_count // n
    depth, hid = weight.shape
    nodes = rows * side
    share = depth // n
    pieces = pieces_of(share)
    piece = share // pieces
    nc = n // 2
    cw = hid // nz
    groups = rows // GROUP
    step_nodes = GROUP * side

    smem = pl.BlockSpec(memory_space=pltpu.SMEM)
    vmem = pl.BlockSpec(memory_space=pltpu.VMEM)
    anywhere = pl.BlockSpec(memory_space=pl.ANY)
    dma = pltpu.SemaphoreType.DMA
    hidden, weight_grad = pl.pallas_call(
        functools.partial(layer_kernel, n, nz),
        out_shape=(
            jax.ShapeDtypeStruct((nodes, hid), jnp.bfloat16),
            jax.ShapeDtypeStruct((share, hid), jnp.float32),
        ),
        in_specs=[smem] * 3 + [anywhere] * 3 + [vmem, anywhere],
        out_specs=(anywhere, vmem),
        scratch_shapes=[
            pltpu.VMEM(feats.shape, jnp.bfloat16),
            pltpu.VMEM(adj.shape, jnp.bfloat16),
            pltpu.VMEM(weight.shape, jnp.bfloat16),
            pltpu.VMEM((nodes, hid), jnp.bfloat16),
            pltpu.VMEM((nodes, hid), jnp.bfloat16),
            pltpu.VMEM((n, 2, rows, width, side), jnp.bfloat16),
            pltpu.VMEM((n, 2, rows, width, side), jnp.bfloat16),
            pltpu.VMEM((tiles, width, side), jnp.float32),
            pltpu.SMEM((block_count,), jnp.int32),
            pltpu.VMEM((depth, nodes), jnp.bfloat16),
            pltpu.VMEM((nodes, hid), jnp.bfloat16),
            pltpu.VMEM((nodes, hid), jnp.float32),
            pltpu.VMEM((step_nodes, depth // 2), jnp.bfloat16),
            pltpu.VMEM((nc * piece, nodes), jnp.bfloat16),
            pltpu.VMEM((nc * piece, hid), jnp.float32),
            pltpu.VMEM((pieces, nc * piece, hid), jnp.bfloat16),
            pltpu.VMEM((pieces, nc * piece, hid), jnp.bfloat16),
            pltpu.VMEM((pieces, piece, hid), jnp.float32),
            pltpu.VMEM((pieces, nc - 1, piece, hid), jnp.bfloat16),
            pltpu.VMEM((pieces, nc - 1, piece, hid), jnp.bfloat16),
            pltpu.VMEM((pieces, piece, hid), jnp.float32),
            pltpu.VMEM((pieces, nz - 1, piece, cw), jnp.bfloat16),
            pltpu.VMEM((pieces, nz - 1, piece, cw), jnp.bfloat16),
            pltpu.VMEM((pieces, piece, cw), jnp.bfloat16),
            pltpu.VMEM((pieces, nz - 1, piece, cw), jnp.bfloat16),
            dma((4,)),
            dma((groups,)),
            dma((n, 1 + groups)),
            dma((n, 1 + groups)),
            dma((pieces, 2)),
            dma((pieces, nc - 1)),
            dma((pieces, nc - 1)),
            dma((pieces, nz - 1)),
            dma((pieces, nz - 1)),
            dma((pieces, nz - 1)),
            dma((pieces, nz - 1)),
        ],
        compiler_params=pltpu.CompilerParams(
            collective_id=0, has_side_effects=True, vmem_limit_bytes=VMEM_BYTES
        ),
        name="layer",
    )(
        tile_rows[0], tile_cols[0], self_blocks[0], feats, adj, weight, proj_bias[None],
        cotangent[0],
    )
    return (hidden[None], weight_grad)


def solution(mesh):
    return jax.shard_map(
        functools.partial(per_device, mesh.shape["feat"], mesh.shape["grp"]),
        mesh=mesh,
        in_specs=(
            P("grp", None, "feat", None),
            P("grp", None, None, None),
            P("grp", None),
            P("grp", None),
            P("grp", None),
            P(),
            P(),
            P("grp", "feat", None),
        ),
        out_specs=(P("grp", "feat", None), P("feat", None)),
        check_vma=False,
    )
```
